512 devices in a mesh: section: 32 (over z, y_hi), tensor: 16 (over x, y_lo, core).
Axes of the slice: x: 4, y: 4 (y_hi: 2, y_lo: 2; y = y_hi * 2 + y_lo), z: 16, core: 2. Of those that a mesh axis runs over, the one named last changes fastest.
Arguments:
- section_input: bfloat16 [32, 128, 4096], P('section', None, 'tensor'), may hold values from -6 to 6
- section_grad: bfloat16 [32, 128, 4096], P('section', None, 'tensor'), may hold values from -6 to 6
- mirror_store: bfloat16 [32, 2, 128, 4096], P('section', None, None, 'tensor'), may hold values from -6 to 6
- fetch_slot: int32 [32], P('section'), may hold values from 0 to 1
- norm_gain: float32 [32, 4096], P('section'), may hold values from 0.25 to 4
- w_query: bfloat16 [32, 4096, 4096], P('section', None, 'tensor')
- w_keyval: bfloat16 [32, 1024, 4096], P('section', 'tensor')
- w_output: bfloat16 [32, 4096, 4096], P('section', 'tensor'), may hold values from -0.09375 to 0.09375
Outputs:
- forward_next: bfloat16 [32, 128, 4096], P('section', None, 'tensor')
- grad_prev: bfloat16 [32, 128, 4096], P('section', None, 'tensor')
- evicted: bfloat16 [32, 128, 4096], P('section', None, 'tensor')
The draws below stay inside these ranges and needn't reach their ends.
All inputs are finite; a program needn't handle non-finite values.
Results may differ from the reference program's by a relative error of at most 0.023.
Values may be sent and summed in bfloat16 or wider, within the bound.
No kernel may reach another device: no remote copies, remote signals or barrier semaphores. Data moves between devices by JAX's collectives and lax.ppermute only.
A program may use at most 64 MiB of HBM per device.

```python
import math
import jax
import jax.numpy as jnp
from jax import lax

D = 4096
HEADS = 32
KV_HEADS = 4
HEAD_DIM = 128
TOKENS = 128
SLOTS = 2
SECTIONS = 32
N_TENSOR = 16


def drawn_base(key):
    values = jax.random.normal(key, (SECTIONS, KV_HEADS * HEAD_DIM, D), jnp.float32)
    return jnp.clip(values, -6.0, 6.0)


def draw_w_keyval(key, part):
    base = drawn_base(key)
    key = jax.random.fold_in(key, 7)
    other = jnp.clip(jax.random.normal(key, (SECTIONS, KV_HEADS * HEAD_DIM, D), jnp.float32), -6.0, 6.0)
    return (jnp.concatenate([base, other], axis=1) * D ** (-0.5)).astype(jnp.bfloat16)


def draw_w_query(key, part):
    key = jax.random.fold_in(key, 9)
    own = jnp.clip(jax.random.normal(key, (SECTIONS, D, HEADS * HEAD_DIM), jnp.float32), -6.0, 6.0)
    return (own * D ** (-0.5)).astype(jnp.bfloat16)


def touch_ends(array, stream_key, low, top_value):
    index_at = [jax.random.randint(jax.random.fold_in(stream_key, axis), (), 0, length) for axis, length in enumerate(array.shape)]
    main_axis = array.shape.index(max(array.shape))
    neighbour = index_at[:main_axis] + [(index_at[main_axis] + 1) % array.shape[main_axis]] + index_at[main_axis + 1:]
    return array.at[tuple(index_at)].set(low).at[tuple(neighbour)].set(top_value)


def levels(own_key, extent, shards, low, high):
    level, own = 1.0, jax.random.fold_in(own_key, 6)
    for dim, shards_of in shards:
        steps = jnp.exp(jax.random.uniform(jax.random.fold_in(own, dim), (shards_of,), jnp.float32, low / len(shards), high / len(shards)))
        level = level * jnp.repeat(steps, extent[dim] // shards_of).reshape([-1 if axis == dim else 1 for axis in range(len(extent))])
    return level


def scatter_about(key, extent, scale, bound, cuts=(), kind=jnp.bfloat16):
    values = scale * jax.random.normal(key, extent, jnp.float32)
    if cuts:
        values = values * levels(key, extent, cuts, -0.22, 0.18)
    return jnp.clip(values, -bound, bound).astype(kind)


def setup_inputs(seed: int = 0) -> dict:
    seeds = jax.random.split(jax.random.key(seed), 9)
    return {
        "section_input": scatter_about(seeds[0], (SECTIONS, TOKENS, D), 1.0, 6.0, ((0, 32), (2, 16))),
        "section_grad": scatter_about(seeds[1], (SECTIONS, TOKENS, D), 1.0, 6.0, ((0, 32), (2, 16))),
        "mirror_store": scatter_about(seeds[2], (SECTIONS, SLOTS, TOKENS, D), 1.0, 6.0, ((0, 32), (3, 16))),
        "fetch_slot": touch_ends(jax.random.randint(seeds[3], (SECTIONS,), 0, SLOTS), jax.random.fold_in(seeds[3], 1), 0, SLOTS - 1).astype(jnp.int32),
        "norm_gain": jnp.clip(jnp.exp(math.log(4.0) - 2.7725887 * jax.random.uniform(seeds[4], (SECTIONS, D), jnp.float32) ** levels(seeds[4], (SECTIONS, D), ((0, 32),), -0.2, 0.2)), 0.25, 4.0),
        "w_query": draw_w_query(jax.random.fold_in(seeds[8], 71), 0),
        "w_keyval": draw_w_keyval(jax.random.fold_in(seeds[8], 71), 0),
        "w_output": scatter_about(seeds[7], (SECTIONS, HEADS * HEAD_DIM, D), (HEADS * HEAD_DIM) ** -0.5, 0.09375, ((0, 32), (1, 16))),
    }


epsilon = 1e-05

def to_bfloat(values):
    return lax.optimization_barrier(values.astype(jnp.bfloat16)).astype(jnp.float32)

def normalize(layer_rows, gain_row):
    widened = layer_rows.astype(jnp.float32)
    inverse = lax.rsqrt(lax.optimization_barrier(jnp.mean(widened * widened, axis=-1, keepdims=True)) + epsilon)
    return (widened * inverse * gain_row).astype(jnp.bfloat16)

def device_sum(terms):
    return lax.optimization_barrier(jnp.sum(to_bfloat(terms), axis=0))

def attend(layer_rows, gain_row, query_w, keyval_w):
    count = layer_rows.shape[0]
    groups = HEADS // KV_HEADS
    normed = normalize(layer_rows, gain_row)
    queries = jnp.dot(normed, query_w, preferred_element_type=jnp.float32).astype(jnp.bfloat16)
    keyvals = lax.dot_general(normed, keyval_w, (((1,), (1,)), ((), ())), preferred_element_type=jnp.float32).astype(jnp.bfloat16)
    query_heads = queries.astype(jnp.float32).reshape(count, HEADS, HEAD_DIM)
    key_heads = keyvals[:, :KV_HEADS * HEAD_DIM].astype(jnp.float32).reshape(count, KV_HEADS, HEAD_DIM)
    value_heads = keyvals[:, KV_HEADS * HEAD_DIM:].astype(jnp.float32).reshape(count, KV_HEADS, HEAD_DIM)
    key_wide = jnp.repeat(key_heads, groups, axis=1)
    value_wide = jnp.repeat(value_heads, groups, axis=1)
    scores = jnp.einsum('thd,shd->hts', query_heads, key_wide) * HEAD_DIM ** (-0.5)
    position = jnp.arange(count, dtype=jnp.int32)
    causal = position[:, None] >= position[None, :]
    scores = jnp.where(causal[None], scores, jnp.float32(-1e+30))
    row_max = lax.optimization_barrier(jnp.max(scores, axis=-1, keepdims=True))
    expval = jnp.exp(scores - row_max)
    probs = expval / lax.optimization_barrier(jnp.sum(expval, axis=-1, keepdims=True))
    return (query_heads, key_wide, value_wide, probs)

def forward_section(layer_rows, gain_row, query_w, keyval_w, output_w):
    count = layer_rows.shape[0]
    block = HEADS * HEAD_DIM // N_TENSOR
    query_heads, key_wide, value_wide, probs = attend(layer_rows, gain_row, query_w, keyval_w)
    mixed = to_bfloat(jnp.einsum('hts,shd->thd', to_bfloat(probs), value_wide)).reshape(count, N_TENSOR, block)
    terms = jnp.einsum('tpk,pkd->ptd', mixed, output_w.astype(jnp.float32).reshape(N_TENSOR, block, D))
    out_sum = device_sum(terms)
    return (layer_rows.astype(jnp.float32) + out_sum).astype(jnp.bfloat16)

def backward_section(layer_rows, grad_rows, gain_row, query_w, keyval_w, output_w):
    count = layer_rows.shape[0]
    block = HEADS * HEAD_DIM // N_TENSOR
    per_dev = HEADS // N_TENSOR
    columns = 2 * KV_HEADS * HEAD_DIM // N_TENSOR
    score_scale = HEAD_DIM ** (-0.5)
    query_heads, key_wide, value_wide, probs = attend(layer_rows, gain_row, query_w, keyval_w)
    grad_wide = grad_rows.astype(jnp.float32)
    dmixed = to_bfloat(jnp.einsum('td,kd->tk', grad_wide, output_w.astype(jnp.float32))).reshape(count, HEADS, HEAD_DIM)
    dprob = jnp.einsum('thd,shd->hts', dmixed, value_wide)
    row_dot = lax.optimization_barrier(jnp.sum(probs * dprob, axis=-1, keepdims=True))
    dscore = to_bfloat(probs * (dprob - row_dot))
    dqueries = to_bfloat(jnp.einsum('hts,shd->thd', dscore, key_wide) * score_scale)
    dkey_heads = jnp.einsum('hts,thd->hsd', dscore, query_heads) * score_scale
    dval_heads = jnp.einsum('hts,thd->hsd', to_bfloat(probs), dmixed)
    share = N_TENSOR // KV_HEADS
    dkey_dev = to_bfloat(dkey_heads.reshape(N_TENSOR, per_dev, count, HEAD_DIM).sum(axis=1))
    dval_dev = to_bfloat(dval_heads.reshape(N_TENSOR, per_dev, count, HEAD_DIM).sum(axis=1))
    dkey = to_bfloat(dkey_dev.reshape(KV_HEADS, share, count, HEAD_DIM).sum(axis=1))
    dval = to_bfloat(dval_dev.reshape(KV_HEADS, share, count, HEAD_DIM).sum(axis=1))
    dkeyvals = jnp.concatenate([jnp.transpose(dkey, (1, 0, 2)).reshape(count, KV_HEADS * HEAD_DIM), jnp.transpose(dval, (1, 0, 2)).reshape(count, KV_HEADS * HEAD_DIM)], axis=1)
    terms = jnp.einsum('tpk,dpk->ptd', dqueries.reshape(count, N_TENSOR, block), query_w.astype(jnp.float32).reshape(D, N_TENSOR, block))
    terms = terms + jnp.einsum('tpc,pcd->ptd', dkeyvals.reshape(count, N_TENSOR, columns), keyval_w.astype(jnp.float32).reshape(N_TENSOR, columns, D))
    dnormed = device_sum(terms)
    widened = layer_rows.astype(jnp.float32)
    inverse = lax.rsqrt(lax.optimization_barrier(jnp.mean(widened * widened, axis=-1, keepdims=True)) + epsilon)
    scaled = gain_row * dnormed
    dlayer = inverse * scaled - widened * inverse ** 3 * lax.optimization_barrier(jnp.mean(widened * scaled, axis=-1, keepdims=True))
    return (grad_wide + dlayer).astype(jnp.bfloat16)

def reference(section_input, section_grad, mirror_store, fetch_slot, norm_gain, w_query, w_keyval, w_output):
    sections = section_input.shape[0]
    section_ids = jnp.arange(sections, dtype=jnp.int32)
    outputs = lax.map(lambda section_id: forward_section(section_input[section_id], norm_gain[section_id], w_query[section_id], w_keyval[section_id], w_output[section_id]), section_ids)
    held_rows = mirror_store[section_ids, fetch_slot]
    fetched = held_rows[::-1]
    gradients = lax.map(lambda section_id: backward_section(fetched[section_id], section_grad[section_id], norm_gain[section_id], w_query[section_id], w_keyval[section_id], w_output[section_id]), section_ids)
    return (jnp.roll(outputs, 1, axis=0), jnp.roll(gradients, -1, axis=0), section_input[::-1])
```

```python
import jax
import jax.numpy as jnp
from jax import lax
from jax.sharding import Mesh, PartitionSpec as P

HEADS = 32
KV_HEADS = 4
HEAD_DIM = 128
EPS = 1e-05
SCALE = HEAD_DIM ** (-0.5)

SEC = ("z", "yh")
TEN = ("x", "yl", "c")
F32 = jnp.float32
BF16 = jnp.bfloat16


def shift(block, distance):
    return lax.ppermute(block, SEC, [(i, (i + distance) % 32) for i in range(32)])


def mirror(block):
    return lax.ppermute(block, SEC, [(i, 31 - i) for i in range(32)])


def swap(block, axis):
    return lax.ppermute(block, axis, [(0, 1), (1, 0)])


def gather(block):
    count, width = block.shape
    spread = jnp.broadcast_to(block, (16, count, width))
    got = lax.all_to_all(spread, TEN, 0, 0, tiled=True)
    return jnp.transpose(got, (1, 0, 2)).reshape(count, 16 * width)


def scatter_sum(term, core):
    count, width = term.shape
    blocks = jnp.transpose(term.astype(BF16).reshape(count, 8, 2, width // 16), (2, 1, 0, 3))
    even, odd = blocks[0], blocks[1]
    keep = jnp.where(core == 0, even, odd)
    away = jnp.where(core == 0, odd, even)
    pair = (keep.astype(F32) + swap(away, "c").astype(F32)).astype(BF16)
    got = lax.all_to_all(pair, ("x", "yl"), 0, 0, tiled=True)
    return got.astype(F32).sum(axis=0)


def head_rows(keyval_w):
    route = []
    for r in range(16):
        half, g = divmod(r // 2, 4)
        route.append((r, 4 * g + 2 * half + r % 2))
    first = lax.ppermute(keyval_w, TEN, route)
    other = swap(first, "yl")
    low = lax.axis_index("yl") == 0
    part = jnp.stack([jnp.where(low, first, other), jnp.where(low, other, first)])
    twin = swap(part, "c")
    even = lax.axis_index("c") == 0
    whole = jnp.stack([jnp.where(even, part, twin), jnp.where(even, twin, part)], axis=1)
    return whole.reshape(4 * keyval_w.shape[0], keyval_w.shape[1])


def project(x, gain, wq, wkv):
    wide = x.astype(F32)
    inv = lax.rsqrt(jnp.mean(wide * wide, axis=-1, keepdims=True) + EPS)
    normed = (wide * inv * gain).astype(BF16)
    q = jnp.dot(normed, wq, preferred_element_type=F32).astype(BF16)
    kv = lax.dot_general(
        normed, wkv, (((1,), (1,)), ((), ())), preferred_element_type=F32
    ).astype(BF16)
    count = x.shape[0]
    qh = q.reshape(count, -1, HEAD_DIM)
    k, v = kv[:, :HEAD_DIM], kv[:, HEAD_DIM:]
    scores = jnp.einsum("thd,sd->hts", qh, k, preferred_element_type=F32) * SCALE
    pos = jnp.arange(count, dtype=jnp.int32)
    scores = jnp.where((pos[:, None] >= pos[None, :])[None], scores, F32(-1e30))
    e = jnp.exp(scores - jnp.max(scores, axis=-1, keepdims=True))
    probs = e / jnp.sum(e, axis=-1, keepdims=True)
    return wide, inv, q, kv, probs


def body(section_input, section_grad, mirror_store, fetch_slot, norm_gain, w_query, w_keyval, w_output):
    x_cols, g_cols = section_input[0], section_grad[0]
    gain, wq, wo = norm_gain[0], w_query[0], w_output[0]
    count = x_cols.shape[0]
    core = lax.axis_index("c")

    fetched = mirror(mirror_store[0][fetch_slot[0]])
    wkv = head_rows(w_keyval[0])
    xg = gather(jnp.concatenate([x_cols, g_cols]))
    x_full, g_full = xg[:count], xg[count:]
    f_full = gather(fetched)
    evicted = mirror(x_cols)

    _, _, _, kv, probs = project(x_full, gain, wq, wkv)
    mixed = jnp.einsum(
        "hts,sd->thd", probs.astype(BF16), kv[:, HEAD_DIM:], preferred_element_type=F32
    ).astype(BF16)
    term = jnp.dot(mixed.reshape(count, -1), wo, preferred_element_type=F32)
    layer_out = (x_cols.astype(F32) + scatter_sum(term, core)).astype(BF16)
    forward_next = shift(layer_out, 1)

    wide, inv, q, kv, probs = project(f_full, gain, wq, wkv)
    qh = q.reshape(count, -1, HEAD_DIM)
    k, v = kv[:, :HEAD_DIM], kv[:, HEAD_DIM:]
    dmixed = lax.dot_general(
        g_full, wo, (((1,), (1,)), ((), ())), preferred_element_type=F32
    ).astype(BF16).reshape(count, -1, HEAD_DIM)
    dprob = jnp.einsum("thd,sd->hts", dmixed, v, preferred_element_type=F32)
    rowdot = jnp.sum(probs * dprob, axis=-1, keepdims=True)
    dscore = (probs * (dprob - rowdot)).astype(BF16)
    dq = (jnp.einsum("hts,sd->thd", dscore, k, preferred_element_type=F32) * SCALE).astype(BF16)
    dk = jnp.einsum("hts,thd->sd", dscore, qh, preferred_element_type=F32) * SCALE
    dv = jnp.einsum("hts,thd->sd", probs.astype(BF16), dmixed, preferred_element_type=F32)
    dkv = jnp.concatenate([dk, dv], axis=1).astype(BF16)
    dterm = lax.dot_general(
        dq.reshape(count, -1), wq, (((1,), (1,)), ((), ())), preferred_element_type=F32
    )
    dterm = gain * (dterm + jnp.dot(dkv, wkv, preferred_element_type=F32))
    stat = jnp.mean(wide * dterm, axis=-1, keepdims=True)
    dterm = inv * dterm - wide * (inv**3 * stat)
    dx = (g_cols.astype(F32) + scatter_sum(dterm, core)).astype(BF16)
    grad_prev = shift(dx, -1)
    return forward_next[None], grad_prev[None], evicted[None]


def solution(mesh):
    fine = Mesh(mesh.devices.reshape(16, 2, 4, 2, 2), SEC + TEN)
    cols = P(SEC, None, TEN)
    return jax.shard_map(
        body,
        mesh=fine,
        in_specs=(
            cols,
            cols,
            P(SEC, None, None, TEN),
            P(SEC),
            P(SEC, None),
            cols,
            P(SEC, TEN, None),
            P(SEC, TEN, None),
        ),
        out_specs=(cols, cols, cols),
        check_vma=False,
    )
```

```python
import jax
import jax.numpy as jnp
from jax import lax
from jax.experimental import pallas as pl
from jax.experimental.pallas import tpu as pltpu
from jax.sharding import Mesh, PartitionSpec as P

HEAD_DIM = 128
EPS = 1e-05
SCALE = HEAD_DIM ** (-0.5)
D = 4096
T = 128
W = 256
N = D // W

SEC = ("z", "yh")
TEN = ("x", "yl", "c")
F32 = jnp.float32
BF16 = jnp.bfloat16
NT = (((1,), (1,)), ((), ()))
TN = (((0,), (0,)), ((), ()))


def dot(a, b, dims=(((1,), (0,)), ((), ()))):
    return lax.dot_general(a, b, dims, preferred_element_type=F32)


def call(kernel, outs, core, *args, scratch=(), flops=0):
    nbytes = sum(a.size * a.dtype.itemsize for a in args)
    return pl.pallas_call(
        kernel,
        out_shape=tuple(pltpu.VMEM(s, d) for s, d in outs),
        in_specs=[pl.BlockSpec(memory_space=pltpu.SMEM)]
        + [pl.BlockSpec(memory_space=pltpu.VMEM)] * len(args),
        out_specs=tuple(pl.BlockSpec(memory_space=pltpu.VMEM) for _ in outs),
        scratch_shapes=list(scratch),
        compiler_params=pltpu.CompilerParams(vmem_limit_bytes=24 * 2**20),
        cost_estimate=pl.CostEstimate(flops=flops, bytes_accessed=nbytes, transcendentals=0),
    )(core, *(pltpu.with_memory_space_constraint(a, pltpu.VMEM) for a in args))


def blocks(core, own, other):
    for ref, side in ((own, core), (other, 1 - core)):
        for j in range(8):
            yield ref.at[j], pl.multiple_of((2 * j + side) * W, W)


def recompute(core, xa, xb, gain, wq, wkv, xg):
    squares = jnp.zeros((T, W), F32)
    for x, at in blocks(core, xa, xb):
        wide = x[...].astype(F32)
        squares += wide * wide
        xg[:, pl.ds(at, W)] = (wide * gain[:, pl.ds(at, W)]).astype(BF16)
    inv = lax.rsqrt(jnp.sum(squares, axis=-1, keepdims=True) * (1.0 / D) + EPS)
    q = dot(xg[...], wq[...]) * inv
    kv = dot(xg[...], wkv[...], NT) * inv
    qb, kvb = q.astype(BF16), kv.astype(BF16)
    k, v = kvb[:, :HEAD_DIM], kvb[:, HEAD_DIM:]
    row = lax.broadcasted_iota(jnp.int32, (T, T), 0)
    col = lax.broadcasted_iota(jnp.int32, (T, T), 1)
    probs = []
    for h in range(2):
        s = dot(qb[:, h * HEAD_DIM : (h + 1) * HEAD_DIM], k, NT) * SCALE
        s = jnp.where(row >= col, s, F32(-1e30))
        e = jnp.exp(s - jnp.max(s, axis=-1, keepdims=True))
        probs.append(e / jnp.sum(e, axis=-1, keepdims=True))
    return inv, q, kv, qb, k, v, probs


def forward_kernel(core_ref, xa, xb, gain, wq, wkv, wo, keep, send, xg):
    core = core_ref[0]
    _, _, _, _, _, v, probs = recompute(core, xa, xb, gain, wq, wkv, xg)
    mixed = jnp.concatenate([dot(p.astype(BF16), v).astype(BF16) for p in probs], axis=1)
    for out, at in blocks(core, keep, send):
        out[...] = dot(mixed, wo[:, pl.ds(at, W)]).astype(BF16)


def dmixed_kernel(core_ref, ga, gb, wo, dmixed, g):
    for block, at in blocks(core_ref[0], ga, gb):
        g[:, pl.ds(at, W)] = block[...]
    dmixed[...] = dot(g[...], wo[...], NT).astype(BF16)


def backward_kernel(core_ref, xa, xb, gain, wq, wkv, dmixed, keep, send, xg):
    core = core_ref[0]
    inv, q, kv, qb, k, v, probs = recompute(core, xa, xb, gain, wq, wkv, xg)
    dq, dk, dv = [], 0.0, 0.0
    for h, p in enumerate(probs):
        lanes = slice(h * HEAD_DIM, (h + 1) * HEAD_DIM)
        dm = dmixed[:, lanes]
        dprob = dot(dm, v, NT)
        rowdot = jnp.sum(p * dprob, axis=-1, keepdims=True)
        dscore = (p * (dprob - rowdot)).astype(BF16)
        dq.append(dot(dscore, k) * SCALE)
        dk += dot(dscore, qb[:, lanes], TN)
        dv += dot(p.astype(BF16), dm, TN)
    dq = jnp.concatenate(dq, axis=1)
    dkv = jnp.concatenate([dk * SCALE, dv], axis=1)
    share = jnp.sum(dq * q + dkv * kv, axis=-1, keepdims=True)
    coef = inv * inv * share * (1.0 / D)
    dqs, dkvs = (dq * inv).astype(BF16), (dkv * inv).astype(BF16)
    for (out, at), (x, _) in zip(blocks(core, keep, send), blocks(core, xa, xb)):
        term = dot(dqs, wq[pl.ds(at, W), :], NT) + dot(dkvs, wkv[:, pl.ds(at, W)])
        term = term * gain[:, pl.ds(at, W)] - coef * x[...].astype(F32)
        out[...] = term.astype(BF16)


def pair_kernel(_, keep, got, out):
    out[...] = (keep[...].astype(F32) + got[...].astype(F32)).astype(BF16)


def finish_kernel(_, base, got, out):
    total = base[...].astype(F32)
    for j in range(8):
        total += got[j].astype(F32)
    out[...] = total.astype(BF16)


def shift(block, distance):
    return lax.ppermute(block, SEC, [(i, (i + distance) % 32) for i in range(32)])


def mirror(block):
    return lax.ppermute(block, SEC, [(i, 31 - i) for i in range(32)])


def swap(block, axis):
    return lax.ppermute(block, axis, [(0, 1), (1, 0)])


def exchange(parts):
    return lax.all_to_all(parts, ("x", "yl"), 0, 0, tiled=True)


def head_rows(keyval_w):
    route = []
    for r in range(16):
        half, g = divmod(r // 2, 4)
        route.append((r, 4 * g + 2 * half + r % 2))
    first = lax.ppermute(keyval_w, TEN, route)
    other = swap(first, "yl")
    low = lax.axis_index("yl") == 0
    part = jnp.stack([jnp.where(low, first, other), jnp.where(low, other, first)])
    twin = swap(part, "c")
    even = lax.axis_index("c") == 0
    whole = jnp.stack([jnp.where(even, part, twin), jnp.where(even, twin, part)], axis=1)
    return whole.reshape(4 * keyval_w.shape[0], keyval_w.shape[1])


def body(section_input, section_grad, mirror_store, fetch_slot, norm_gain, w_query, w_keyval, w_output):
    x_cols, g_cols = section_input[0], section_grad[0]
    gain, wq, wo = norm_gain, w_query[0], w_output[0]
    core = lax.axis_index("c").astype(jnp.int32).reshape(1)
    half = ((8, T, W), BF16)
    xg = pltpu.VMEM((T, D), BF16)

    def gather(*blocks):
        spread = jnp.broadcast_to(jnp.stack(blocks), (8, len(blocks), T, W))
        own = exchange(spread)
        other = swap(own, "c")
        return [(own[:, i], other[:, i]) for i in range(len(blocks))]

    def total(base, keep, send):
        (pair,) = call(pair_kernel, [half], core, keep, swap(send, "c"))
        (out,) = call(finish_kernel, [((T, W), BF16)], core, base, exchange(pair))
        return out

    fetched = mirror(mirror_store[0][fetch_slot[0]])
    wkv = head_rows(w_keyval[0])
    ((xa, xb),) = gather(x_cols)
    ((ga, gb),) = gather(g_cols)
    ((fa, fb),) = gather(fetched)
    x_late, fa = lax.optimization_barrier((x_cols, fa))
    evicted = mirror(x_late)

    keep, send = call(
        forward_kernel, [half, half], core, xa, xb, gain, wq, wkv, wo, scratch=[xg], flops=10**9
    )
    forward_next = shift(total(x_cols, keep, send), 1)

    (dmixed,) = call(
        dmixed_kernel, [((T, W), BF16)], core, ga, gb, wo, scratch=[xg], flops=5 * 10**8
    )
    keep, send = call(
        backward_kernel, [half, half], core, fa, fb, gain, wq, wkv, dmixed, scratch=[xg], flops=10**9
    )
    grad_prev = shift(total(g_cols, keep, send), -1)
    return forward_next[None], grad_prev[None], evicted[None]


def solution(mesh):
    fine = Mesh(mesh.devices.reshape(16, 2, 4, 2, 2), SEC + TEN)
    cols = P(SEC, None, TEN)
    return jax.shard_map(
        body,
        mesh=fine,
        in_specs=(
            cols,
            cols,
            P(SEC, None, None, TEN),
            P(SEC),
            P(SEC, None),
            cols,
            P(SEC, TEN, None),
            P(SEC, TEN, None),
        ),
        out_specs=(cols, cols, cols),
        check_vma=False,
    )
```

```python
import jax
import jax.numpy as jnp
from jax import lax
from jax.experimental import pallas as pl
from jax.experimental.pallas import tpu as pltpu
from jax.sharding import Mesh, PartitionSpec as P

HEAD_DIM = 128
EPS = 1e-05
SCALE = HEAD_DIM ** (-0.5)
D = 4096
T = 128
W = 256
N = D // W

SEC = ("z", "yh")
TEN = ("x", "yl", "c")
F32 = jnp.float32
BF16 = jnp.bfloat16
NT = (((1,), (1,)), ((), ()))
TN = (((0,), (0,)), ((), ()))


def dot(a, b, dims=(((1,), (0,)), ((), ()))):
    return lax.dot_general(a, b, dims, preferred_element_type=F32)


def call(kernel, outs, core, *args, after=(), scratch=(), flops=0):
    nbytes = sum(a.size * a.dtype.itemsize for a in args)

    def ordered(core_ref, *refs):
        kernel(core_ref, *refs[: len(args)], *refs[len(args) + len(after) :])

    return pl.pallas_call(
        ordered,
        out_shape=tuple(pltpu.VMEM(s, d) for s, d in outs),
        in_specs=[pl.BlockSpec(memory_space=pltpu.SMEM)]
        + [pl.BlockSpec(memory_space=pltpu.VMEM)] * len(args)
        + [pl.BlockSpec(memory_space=pl.ANY)] * len(after),
        out_specs=tuple(pl.BlockSpec(memory_space=pltpu.VMEM) for _ in outs),
        scratch_shapes=list(scratch),
        compiler_params=pltpu.CompilerParams(vmem_limit_bytes=24 * 2**20),
        cost_estimate=pl.CostEstimate(flops=flops, bytes_accessed=nbytes, transcendentals=0),
    )(core, *(pltpu.with_memory_space_constraint(a, pltpu.VMEM) for a in args), *after)


def blocks(core, own, other, which=0):
    for ref, side in ((own, core), (other, 1 - core)):
        for j in range(8):
            yield ref.at[j, which], pl.multiple_of((2 * j + side) * W, W)


def recompute(core, xa, xb, which, gain, wq, wkv, xg):
    squares = jnp.zeros((T, W), F32)
    for x, at in blocks(core, xa, xb, which):
        wide = x[...].astype(F32)
        squares += wide * wide
        xg[:, pl.ds(at, W)] = (wide * gain[:, pl.ds(at, W)]).astype(BF16)
    inv = lax.rsqrt(jnp.sum(squares, axis=-1, keepdims=True) * (1.0 / D) + EPS)
    q = dot(xg[...], wq[...]) * inv
    kv = dot(xg[...], wkv[...], NT) * inv
    qb, kvb = q.astype(BF16), kv.astype(BF16)
    k, v = kvb[:, :HEAD_DIM], kvb[:, HEAD_DIM:]
    row = lax.broadcasted_iota(jnp.int32, (T, T), 0)
    col = lax.broadcasted_iota(jnp.int32, (T, T), 1)
    probs = []
    for h in range(2):
        s = dot(qb[:, h * HEAD_DIM : (h + 1) * HEAD_DIM], k, NT) * SCALE
        s = jnp.where(row >= col, s, F32(-1e30))
        e = jnp.exp(s - jnp.max(s, axis=-1, keepdims=True))
        probs.append(e / jnp.sum(e, axis=-1, keepdims=True))
    return inv, q, kv, qb, k, v, probs


def forward_kernel(core_ref, xa, xb, gain, wq, wkv, wo, keep, send, xg):
    core = core_ref[0]
    _, _, _, _, _, v, probs = recompute(core, xa, xb, 0, gain, wq, wkv, xg)
    mixed = jnp.concatenate([dot(p.astype(BF16), v).astype(BF16) for p in probs], axis=1)
    for out, at in blocks(core, keep, send):
        out[...] = dot(mixed, wo[:, pl.ds(at, W)]).astype(BF16)


def dmixed_kernel(core_ref, ga, gb, wo, dmixed, g):
    for block, at in blocks(core_ref[0], ga, gb):
        g[:, pl.ds(at, W)] = block[...]
    dmixed[...] = dot(g[...], wo[...], NT).astype(BF16)


def backward_kernel(core_ref, xa, xb, gain, wq, wkv, dmixed, keep, send, xg):
    core = core_ref[0]
    inv, q, kv, qb, k, v, probs = recompute(core, xa, xb, 1, gain, wq, wkv, xg)
    dq, dk, dv = [], 0.0, 0.0
    for h, p in enumerate(probs):
        lanes = slice(h * HEAD_DIM, (h + 1) * HEAD_DIM)
        dm = dmixed[:, lanes]
        dprob = dot(dm, v, NT)
        rowdot = jnp.sum(p * dprob, axis=-1, keepdims=True)
        dscore = (p * (dprob - rowdot)).astype(BF16)
        dq.append(dot(dscore, k) * SCALE)
        dk += dot(dscore, qb[:, lanes], TN)
        dv += dot(p.astype(BF16), dm, TN)
    dq = jnp.concatenate(dq, axis=1)
    dkv = jnp.concatenate([dk * SCALE, dv], axis=1)
    share = jnp.sum(dq * q + dkv * kv, axis=-1, keepdims=True)
    coef = inv * inv * share * (1.0 / D)
    dqs, dkvs = (dq * inv).astype(BF16), (dkv * inv).astype(BF16)
    for (out, at), (x, _) in zip(blocks(core, keep, send), blocks(core, xa, xb, 1)):
        term = dot(dqs, wq[pl.ds(at, W), :], NT) + dot(dkvs, wkv[:, pl.ds(at, W)])
        term = term * gain[:, pl.ds(at, W)] - coef * x[...].astype(F32)
        out[...] = term.astype(BF16)


def spread_kernel(_, *refs):
    *blocks_in, out = refs
    for i, block in enumerate(blocks_in):
        for j in range(8):
            out[j, i] = block[...]


def copy_kernel(_, block, out):
    out[...] = block[...]


def assemble_kernel(place, first, other, twin_first, twin_other, out):
    core, low = place[0], place[1]
    rows = first.shape[0]
    for ref, half, side in (
        (first, low, core),
        (other, 1 - low, core),
        (twin_first, low, 1 - core),
        (twin_other, 1 - low, 1 - core),
    ):
        out[pl.ds(pl.multiple_of((2 * half + side) * rows, rows), rows), :] = ref[...]


def pair_kernel(_, keep, got, out):
    out[...] = (keep[...].astype(F32) + got[...].astype(F32)).astype(BF16)


def finish_kernel(_, base, got, out):
    total = base[...].astype(F32)
    for j in range(8):
        total += got[j, 0].astype(F32)
    out[...] = total.astype(BF16)


def shift(block, distance):
    return lax.ppermute(block, SEC, [(i, (i + distance) % 32) for i in range(32)])


def mirror(block):
    return lax.ppermute(block, SEC, [(i, 31 - i) for i in range(32)])


def swap(block, axis):
    return lax.ppermute(block, axis, [(0, 1), (1, 0)])


def exchange(parts):
    return lax.all_to_all(parts, ("x", "yl"), 0, 0, tiled=True)


def body(section_input, section_grad, mirror_store, fetch_slot, norm_gain, w_query, w_keyval, w_output):
    x_cols, g_cols = section_input[0], section_grad[0]
    gain, wq, wo, keyval_w = norm_gain, w_query[0], w_output[0], w_keyval[0]
    core = lax.axis_index("c").astype(jnp.int32).reshape(1)
    place = jnp.stack([lax.axis_index("c"), lax.axis_index("yl")]).astype(jnp.int32)
    tile = ((T, W), BF16)
    half = ((8, 1, T, W), BF16)
    xg = pltpu.VMEM((T, D), BF16)

    def gather(*parts, after=()):
        n = len(parts)
        (spread,) = call(spread_kernel, [((8, n, T, W), BF16)], core, *parts, after=after)
        own = exchange(spread)
        return own, swap(own, "c")

    def total(base, keep, send, after=()):
        (pair,) = call(pair_kernel, [half], core, keep, swap(send, "c"), after=after)
        (out,) = call(finish_kernel, [tile], core, base, exchange(pair))
        return out

    fetched = mirror(mirror_store[0][fetch_slot[0]])

    route = []
    for r in range(16):
        part, g = divmod(r // 2, 4)
        route.append((r, 4 * g + 2 * part + r % 2))
    first = lax.ppermute(keyval_w, TEN, route)
    (first,) = call(copy_kernel, [(first.shape, BF16)], core, first, after=(fetched,))
    other = swap(first, "yl")
    (wkv,) = call(
        assemble_kernel, [((W, D), BF16)], place, first, other, swap(first, "c"), swap(other, "c")
    )

    ga, gb = gather(g_cols)
    xa, xb = gather(x_cols, fetched)
    (x_late,) = call(copy_kernel, [tile], core, x_cols, after=(fetched,))
    evicted = mirror(x_late)

    keep, send = call(
        forward_kernel, [half, half], core, xa, xb, gain, wq, wkv, wo, scratch=[xg], flops=10**9
    )
    forward_next = shift(total(x_cols, keep, send, after=(evicted,)), 1)

    (dmixed,) = call(dmixed_kernel, [tile], core, ga, gb, wo, scratch=[xg], flops=5 * 10**8)
    keep, send = call(
        backward_kernel, [half, half], core, xa, xb, gain, wq, wkv, dmixed, scratch=[xg], flops=10**9
    )
    grad_prev = shift(total(g_cols, keep, send), -1)
    return forward_next[None], grad_prev[None], evicted[None]


def solution(mesh):
    fine = Mesh(mesh.devices.reshape(16, 2, 4, 2, 2), SEC + TEN)
    cols = P(SEC, None, TEN)
    return jax.shard_map(
        body,
        mesh=fine,
        in_specs=(
            cols,
            cols,
            P(SEC, None, None, TEN),
            P(SEC),
            P(SEC, None),
            cols,
            P(SEC, TEN, None),
            P(SEC, TEN, None),
        ),
        out_specs=(cols, cols, cols),
        check_vma=False,
    )
```

```python
import jax
import jax.numpy as jnp
from jax import lax
from jax.experimental import pallas as pl
from jax.experimental.pallas import tpu as pltpu
from jax.sharding import Mesh, PartitionSpec as P

HEAD_DIM = 128
EPS = 1e-05
SCALE = HEAD_DIM ** (-0.5)
D = 4096
T = 128
W = 256
N = D // W

SEC = ("z", "yh")
TEN = ("x", "yl", "c")
F32 = jnp.float32
BF16 = jnp.bfloat16
NT = (((1,), (1,)), ((), ()))
TN = (((0,), (0,)), ((), ()))


def dot(a, b, dims=(((1,), (0,)), ((), ()))):
    return lax.dot_general(a, b, dims, preferred_element_type=F32)


def call(kernel, outs, core, *args, after=(), scratch=(), flops=0):
    nbytes = sum(a.size * a.dtype.itemsize for a in args)

    def ordered(core_ref, *refs):
        kernel(core_ref, *refs[: len(args)], *refs[len(args) + len(after) :])

    return pl.pallas_call(
        ordered,
        out_shape=tuple(pltpu.VMEM(s, d) for s, d in outs),
        in_specs=[pl.BlockSpec(memory_space=pltpu.SMEM)]
        + [pl.BlockSpec(memory_space=pltpu.VMEM)] * len(args)
        + [pl.BlockSpec(memory_space=pl.ANY)] * len(after),
        out_specs=tuple(pl.BlockSpec(memory_space=pltpu.VMEM) for _ in outs),
        scratch_shapes=list(scratch),
        compiler_params=pltpu.CompilerParams(vmem_limit_bytes=24 * 2**20),
        cost_estimate=pl.CostEstimate(flops=flops, bytes_accessed=nbytes, transcendentals=0),
    )(core, *(pltpu.with_memory_space_constraint(a, pltpu.VMEM) for a in args), *after)


def in_hbm(a):
    return pltpu.with_memory_space_constraint(a, pltpu.HBM)


def blocks(core, own, other, which=0):
    for ref, side in ((own, core), (other, 1 - core)):
        for j in range(8):
            yield ref.at[j, which], pl.multiple_of((2 * j + side) * W, W)


def load_kernel(slot, store, x, g, held_out, x_out, g_out, sems):
    copies = [
        pltpu.make_async_copy(store.at[0, slot[0]], held_out, sems.at[0]),
        pltpu.make_async_copy(x.at[0], x_out, sems.at[1]),
        pltpu.make_async_copy(g.at[0], g_out, sems.at[2]),
    ]
    for copy in copies:
        copy.start()
    for copy in copies:
        copy.wait()


def spread_kernel(_, x, fetched, g, out):
    for j in range(8):
        out[j, 0] = x[...]
        out[j, 1] = fetched[...]
        out[j, 2] = g[...]


def assemble_kernel(core, first, twin, out):
    rows = first.shape[0]
    for ref, side in ((first, core[0]), (twin, 1 - core[0])):
        out[pl.ds(pl.multiple_of(side * rows, rows), rows), :] = ref[...]


def keyval_kernel(core_ref, own, other, gain, wkv, xg, inv_out, kv_out, kvb_out):
    for which in range(2):
        rows = slice(which * T, (which + 1) * T)
        squares = jnp.zeros((T, W), F32)
        for x, at in blocks(core_ref[0], own, other, which):
            wide = x[...].astype(F32)
            squares += wide * wide
            xg[rows, pl.ds(at, W)] = (wide * gain[:, pl.ds(at, W)]).astype(BF16)
        mean = jnp.sum(squares, axis=-1, keepdims=True) * (1.0 / D)
        inv_out[rows, :] = lax.rsqrt(mean + EPS)
    kv = dot(xg[...], wkv[...], NT) * inv_out[...]
    kv_out[...] = kv
    kvb_out[...] = kv.astype(BF16)


def queries_kernel(core_ref, own, other, xg, inv, wq, wo, q_out, dmixed, g):
    q_out[...] = dot(xg[...], wq[...]) * inv[...]
    for block, at in blocks(core_ref[0], own, other, 2):
        g[:, pl.ds(at, W)] = block[...]
    dmixed[...] = dot(g[...], wo[...], NT).astype(BF16)


def attend_kernel(low_ref, kvb, got, q, dmixed, mixed, dq_out, own_out, away_out):
    low = low_ref[0] == 0
    row = lax.broadcasted_iota(jnp.int32, (T, T), 0)
    col = lax.broadcasted_iota(jnp.int32, (T, T), 1)
    dk, dv = 0.0, 0.0
    for which in range(2):
        rows = slice(which * T, (which + 1) * T)
        k = jnp.where(low, kvb[rows, :], got[rows, :])
        v = jnp.where(low, got[rows, :], kvb[rows, :])
        for h in range(2):
            lanes = slice(h * HEAD_DIM, (h + 1) * HEAD_DIM)
            qb = q[rows, lanes].astype(BF16)
            s = dot(qb, k, NT) * SCALE
            s = jnp.where(row >= col, s, F32(-1e30))
            e = jnp.exp(s - jnp.max(s, axis=-1, keepdims=True))
            p = e / jnp.sum(e, axis=-1, keepdims=True)
            pb = p.astype(BF16)
            if which == 0:
                mixed[:, lanes] = dot(pb, v).astype(BF16)
                continue
            dm = dmixed[:, lanes]
            dprob = dot(dm, v, NT)
            dscore = (p * (dprob - jnp.sum(p * dprob, axis=-1, keepdims=True))).astype(BF16)
            dq_out[:, lanes] = dot(dscore, k) * SCALE
            dk += dot(dscore, qb, TN)
            dv += dot(pb, dm, TN)
    dk = dk * SCALE
    own_out[...] = jnp.where(low, dk, dv)
    away_out[...] = jnp.where(low, dv, dk).astype(BF16)


def output_kernel(core_ref, mixed, wo, keep, send):
    for out, at in blocks(core_ref[0], keep, send):
        out[...] = dot(mixed[...], wo[:, pl.ds(at, W)]).astype(BF16)


def input_kernel(core_ref, own, other, gain, wq, wkv, inv, q, kv, dq, mine, got, keep, send):
    core = core_ref[0]
    r = inv[T:, :]
    dkv = mine[...] + got[...].astype(F32)
    share = jnp.sum(dq[...] * q[T:, :], axis=-1, keepdims=True)
    share += jnp.sum(dkv * kv[T:, :], axis=-1, keepdims=True)
    coef = r * r * share * (1.0 / D)
    dqs, dkvs = (dq[...] * r).astype(BF16), (dkv * r).astype(BF16)
    for (out, at), (x, _) in zip(blocks(core, keep, send), blocks(core, own, other, 1)):
        term = dot(dqs, wq[pl.ds(at, W), :], NT) + dot(dkvs, wkv[:, pl.ds(at, W)])
        term = term * gain[:, pl.ds(at, W)] - coef * x[...].astype(F32)
        out[...] = term.astype(BF16)


def pair_kernel(_, keep_y, got_y, keep_dx, got_dx, x, out, x_out):
    for j in range(8):
        out[j, 0] = (keep_y[j, 0].astype(F32) + got_y[j, 0].astype(F32)).astype(BF16)
        out[j, 1] = (keep_dx[j, 0].astype(F32) + got_dx[j, 0].astype(F32)).astype(BF16)
    x_out[...] = x[...]


def finish_kernel(_, x, g, got, y_out, dx_out):
    for which, base, out in ((0, x, y_out), (1, g, dx_out)):
        total = base[...].astype(F32)
        for j in range(8):
            total += got[j, which].astype(F32)
        out[...] = total.astype(BF16)


def shift(block, distance):
    return lax.ppermute(block, SEC, [(i, (i + distance) % 32) for i in range(32)])


def mirror(block):
    return lax.ppermute(block, SEC, [(i, 31 - i) for i in range(32)])


def swap(block, axis):
    return lax.ppermute(block, axis, [(0, 1), (1, 0)])


def exchange(parts):
    return lax.all_to_all(parts, ("x", "yl"), 0, 0, tiled=True)


def body(section_input, section_grad, mirror_store, fetch_slot, norm_gain, w_query, w_keyval, w_output):
    gain, wq, wo, keyval_w = norm_gain, w_query[0], w_output[0], w_keyval[0]
    core = lax.axis_index("c").astype(jnp.int32).reshape(1)
    low = lax.axis_index("yl").astype(jnp.int32).reshape(1)
    tile = ((T, W), BF16)
    half = ((8, 1, T, W), BF16)

    held, x, g = pl.pallas_call(
        load_kernel,
        out_shape=tuple(pltpu.VMEM((T, W), BF16) for _ in range(3)),
        in_specs=[pl.BlockSpec(memory_space=pltpu.SMEM)]
        + [pl.BlockSpec(memory_space=pl.ANY)] * 3,
        out_specs=tuple(pl.BlockSpec(memory_space=pltpu.VMEM) for _ in range(3)),
        scratch_shapes=[pltpu.SemaphoreType.DMA((3,))],
    )(fetch_slot, *(in_hbm(a) for a in (mirror_store, section_input, section_grad)))
    fetched = mirror(held)

    route = []
    for r in range(16):
        part, group = divmod(r // 2, 4)
        route.append((r, 4 * group + 2 * part + r % 2))
    first = lax.ppermute(keyval_w, TEN, route)
    (wkv,) = call(assemble_kernel, [((HEAD_DIM, D), BF16)], core, first, swap(first, "c"))

    (spread,) = call(spread_kernel, [((8, 3, T, W), BF16)], core, x, fetched, g, after=(first,))
    own = exchange(spread)
    other = swap(own, "c")

    xg, inv, kv, kvb = call(
        keyval_kernel,
        [((2 * T, D), BF16), ((2 * T, 1), F32), ((2 * T, HEAD_DIM), F32), ((2 * T, HEAD_DIM), BF16)],
        core,
        own,
        other,
        gain,
        wkv,
    )
    q, dmixed = call(
        queries_kernel,
        [((2 * T, W), F32), tile],
        core,
        own,
        other,
        xg,
        inv,
        wq,
        wo,
        scratch=[pltpu.VMEM((T, D), BF16)],
        flops=10**9,
    )
    mixed, dq, mine, away = call(
        attend_kernel,
        [tile, ((T, W), F32), ((T, HEAD_DIM), F32), ((T, HEAD_DIM), BF16)],
        low,
        kvb,
        swap(kvb, "yl"),
        q,
        dmixed,
    )
    keep_y, send_y = call(output_kernel, [half, half], core, mixed, wo, flops=10**9)
    keep_dx, send_dx = call(
        input_kernel,
        [half, half],
        core,
        own,
        other,
        gain,
        wq,
        wkv,
        inv,
        q,
        kv,
        dq,
        mine,
        swap(away, "yl"),
    )
    pair, x_late = call(
        pair_kernel,
        [((8, 2, T, W), BF16), tile],
        core,
        keep_y,
        swap(send_y, "c"),
        keep_dx,
        swap(send_dx, "c"),
        x,
    )
    y, dx = call(finish_kernel, [tile, tile], core, x, g, exchange(pair))
    forward_next, grad_prev = shift(y, 1), shift(dx, -1)
    evicted = mirror(x_late)
    return forward_next[None], grad_prev[None], evicted[None]


def solution(mesh):
    fine = Mesh(mesh.devices.reshape(16, 2, 4, 2, 2), SEC + TEN)
    cols = P(SEC, None, TEN)
    return jax.shard_map(
        body,
        mesh=fine,
        in_specs=(
            cols,
            cols,
            P(SEC, None, None, TEN),
            P(SEC),
            P(SEC, None),
            cols,
            P(SEC, TEN, None),
            P(SEC, TEN, None),
        ),
        out_specs=(cols, cols, cols),
        check_vma=False,
    )
```

```python
import jax
import jax.numpy as jnp
from jax import lax
from jax.experimental import pallas as pl
from jax.experimental.pallas import tpu as pltpu
from jax.sharding import Mesh, PartitionSpec as P

HEAD_DIM = 128
EPS = 1e-05
SCALE = HEAD_DIM ** (-0.5)
D = 4096
T = 128
W = 256
N = D // W
PAD = 16

SEC = ("z", "yh")
TEN = ("x", "yl", "c")
F32 = jnp.float32
BF16 = jnp.bfloat16
NT = (((1,), (1,)), ((), ()))
TN = (((0,), (0,)), ((), ()))


def dot(a, b, dims=(((1,), (0,)), ((), ()))):
    return lax.dot_general(a, b, dims, preferred_element_type=F32)


def call(kernel, outs, place, *args, after=(), anywhere=(), scratch=(), flops=0):
    nbytes = sum(a.size * a.dtype.itemsize for a in args)
    n = len(args) + len(anywhere)

    def ordered(core, low, *refs):
        kernel(core, low, *refs[:n], *refs[n + len(after) :])

    return pl.pallas_call(
        ordered,
        out_shape=tuple(pltpu.VMEM(s, d) for s, d in outs),
        in_specs=[pl.BlockSpec(memory_space=pltpu.SMEM)] * 2
        + [pl.BlockSpec(memory_space=pltpu.VMEM)] * len(args)
        + [pl.BlockSpec(memory_space=pl.ANY)] * (len(anywhere) + len(after)),
        out_specs=tuple(pl.BlockSpec(memory_space=pltpu.VMEM) for _ in outs),
        scratch_shapes=list(scratch),
        compiler_params=pltpu.CompilerParams(vmem_limit_bytes=16 * 2**20),
        cost_estimate=pl.CostEstimate(flops=flops, bytes_accessed=nbytes, transcendentals=0),
    )(*place, *(pltpu.with_memory_space_constraint(a, pltpu.VMEM) for a in args), *anywhere, *after)


def in_hbm(a):
    return pltpu.with_memory_space_constraint(a, pltpu.HBM)


def at(index, size=W):
    return pl.ds(pl.multiple_of(index * size, size), size)


def load_kernel(slot, store, x, g, held, x_out, g_out, sems):
    copies = [
        pltpu.make_async_copy(store.at[0, slot[0]], held.at[:T, :], sems.at[0]),
        pltpu.make_async_copy(x.at[0], x_out, sems.at[1]),
        pltpu.make_async_copy(g.at[0], g_out, sems.at[2]),
    ]
    for copy in copies:
        copy.start()
    held[T:, :] = jnp.zeros((PAD, W), BF16)
    for copy in copies:
        copy.wait()


def trade_kernel(core, low, x, g, base, away):
    @pl.when(core[0] == 0)
    def _():
        base[...] = x[...]
        away[...] = g[...]

    @pl.when(core[0] == 1)
    def _():
        base[...] = g[...]
        away[...] = x[...]


def spread_kernel(core, low, base, twin, fetched, out):
    for j in range(8):
        out[j, core[0]] = base[...]
        out[j, 1 - core[0]] = twin[...]
        out[j, 2] = fetched[:T, :]


def pick_kernel(core, low, own, out):
    out[...] = own[:, 2]


def keyval_kernel(
    core, low, own, even, gain, first, twin, xg, inv_out, kv_out, kvb_out, wkv, squares, sems
):
    half = first.shape[0]
    copies = []
    for i, (ref, side) in enumerate(((first, core[0]), (twin, 1 - core[0]))):
        copies.append(pltpu.make_async_copy(ref, wkv.at[at(side, half), :], sems.at[i]))
        copies[i].start()

    def scaled(left, right):
        total = jnp.zeros((T, W), F32)
        for j in range(8):
            for side, block in enumerate((left(j), right(j))):
                here = slice((2 * j + side) * W, (2 * j + side + 1) * W)
                wide = block.astype(F32)
                total += wide * wide
                xg[:, here] = (wide * gain[:, here]).astype(BF16)
        squares[...] = total

    @pl.when(core[0] == 0)
    def _():
        scaled(lambda j: own[j, 0], lambda j: own[j, 1])

    @pl.when(core[0] == 1)
    def _():
        scaled(lambda j: even[j], lambda j: own[j, 2])

    inv = lax.rsqrt(jnp.sum(squares[...], axis=-1, keepdims=True) * (1.0 / D) + EPS)
    inv_out[...] = inv
    for copy in copies:
        copy.wait()
    kv = dot(xg[...], wkv[...], NT) * inv
    kv_out[...] = kv
    kvb_out[...] = kv.astype(BF16)


def loads(weights, refs, sems):
    copies = [pltpu.make_async_copy(w, refs.at[i], sems.at[i]) for i, w in enumerate(weights)]
    for copy in copies:
        copy.start()
    return copies


def queries_kernel(core, low, xg, inv, wq, wq2, q_out, rows, sems):
    for i, load in enumerate(loads((wq, wq2), rows, sems)):
        load.wait()
        q_out[:, i * W : (i + 1) * W] = dot(xg[...], rows[i]) * inv[...]


def dmixed_kernel(core, low, own, wo, wo2, dmixed, cols, g, sems):
    copies = loads((wo, wo2), cols, sems)

    @pl.when(core[0] == 1)
    def _():
        for r in range(N):
            g[:, r * W : (r + 1) * W] = own[r // 2, r % 2]

    for i, copy in enumerate(copies):
        copy.wait()

        @pl.when(core[0] == 1)
        def _(i=i):
            dmixed[:, i * W : (i + 1) * W] = dot(g[...], cols[i], NT).astype(BF16)


def softmax(qb, k):
    row = lax.broadcasted_iota(jnp.int32, (T, T), 0)
    col = lax.broadcasted_iota(jnp.int32, (T, T), 1)
    s = jnp.where(row >= col, dot(qb, k, NT) * SCALE, F32(-1e30))
    e = jnp.exp(s - jnp.max(s, axis=-1, keepdims=True))
    return e / jnp.sum(e, axis=-1, keepdims=True)


def attend_kernel(core, low, kvb, got, q, dmixed, mixed, dq_out, own_out, away_out):
    keys = low[0] == 0
    k = jnp.where(keys, kvb[...], got[...])
    v = jnp.where(keys, got[...], kvb[...])

    @pl.when(core[0] == 0)
    def _():
        for h in range(4):
            lanes = slice(h * HEAD_DIM, (h + 1) * HEAD_DIM)
            p = softmax(q[:, lanes].astype(BF16), k)
            mixed[:, lanes] = dot(p.astype(BF16), v).astype(BF16)
        away_out[...] = jnp.zeros((T, HEAD_DIM), BF16)

    @pl.when(core[0] == 1)
    def _():
        dk, dv = 0.0, 0.0
        for h in range(4):
            lanes = slice(h * HEAD_DIM, (h + 1) * HEAD_DIM)
            qb, dm = q[:, lanes].astype(BF16), dmixed[:, lanes]
            p = softmax(qb, k)
            dprob = dot(dm, v, NT)
            dscore = (p * (dprob - jnp.sum(p * dprob, axis=-1, keepdims=True))).astype(BF16)
            dq_out[:, lanes] = dot(dscore, k) * SCALE
            dk += dot(dscore, qb, TN)
            dv += dot(p.astype(BF16), dm, TN)
        dk = dk * SCALE
        own_out[...] = jnp.where(keys, dk, dv)
        away_out[...] = jnp.where(keys, dv, dk).astype(BF16)


def terms_kernel(
    core, low, own, even, gain, wkv, rows, cols, inv, q, kv, mixed, dq, mine, got, x, out, x_out
):
    x_out[...] = x[...]

    @pl.when(core[0] == 0)
    def _():
        for r in range(N):
            here = slice(r * W, (r + 1) * W)
            term = dot(mixed[:, :W], cols[0, :, here]) + dot(mixed[:, W:], cols[1, :, here])
            out[r // 2, r % 2] = term.astype(BF16)

    @pl.when(core[0] == 1)
    def _():
        r_norm = inv[...]
        dkv = mine[...] + got[...].astype(F32)
        share = jnp.sum(dq[...] * q[...], axis=-1, keepdims=True)
        share += jnp.sum(dkv * kv[...], axis=-1, keepdims=True)
        coef = r_norm * r_norm * share * (1.0 / D)
        dqs, dkvs = (dq[...] * r_norm).astype(BF16), (dkv * r_norm).astype(BF16)
        for r in range(N):
            here = slice(r * W, (r + 1) * W)
            f = own[r // 2, 2] if r % 2 else even[r // 2]
            term = dot(dqs[:, :W], rows[0, here, :], NT) + dot(dqs[:, W:], rows[1, here, :], NT)
            term += dot(dkvs, wkv[:, here])
            out[r // 2, r % 2] = (term * gain[:, here] - coef * f.astype(F32)).astype(BF16)


def finish_kernel(core, low, base, twin, got, same, cross):
    for start, side, out in ((base, core[0], same), (twin, 1 - core[0], cross)):
        total = start[...].astype(F32)
        for j in range(8):
            total += got[j, side].astype(F32)
        out[...] = total.astype(BF16)


def store_kernel(core, same, cross, evicted, y_out, dx_out, evicted_out, sems):
    last = pltpu.make_async_copy(evicted, evicted_out.at[0], sems.at[2])
    last.start()

    @pl.when(core[0] == 0)
    def _():
        pltpu.make_async_copy(same, y_out.at[0], sems.at[0]).start()
        pltpu.make_async_copy(cross, dx_out.at[0], sems.at[1]).start()

    @pl.when(core[0] == 1)
    def _():
        pltpu.make_async_copy(cross, y_out.at[0], sems.at[0]).start()
        pltpu.make_async_copy(same, dx_out.at[0], sems.at[1]).start()

    pltpu.make_async_copy(same, y_out.at[0], sems.at[0]).wait()
    pltpu.make_async_copy(cross, dx_out.at[0], sems.at[1]).wait()
    last.wait()


def deliver(block, cross):
    route = []
    for i in range(32):
        route.append((2 * i, 2 * ((i + 1) % 32) + cross))
        route.append((2 * i + 1, 2 * ((i - 1) % 32) + 1 - cross))
    return lax.ppermute(block, SEC + ("c",), route)


def mirror(block):
    return lax.ppermute(block, SEC, [(i, 31 - i) for i in range(32)])


def swap(block, axis):
    return lax.ppermute(block, axis, [(0, 1), (1, 0)])


def exchange(parts):
    return lax.all_to_all(parts, ("x", "yl"), 0, 0, tiled=True)


def body(section_input, section_grad, mirror_store, fetch_slot, norm_gain, w_query, w_keyval, w_output):
    gain, wq, wo, keyval_w = norm_gain, w_query[0], w_output[0], w_keyval[0]
    place = [lax.axis_index(a).astype(jnp.int32).reshape(1) for a in ("c", "yl")]
    tile = ((T, W), BF16)
    wide = ((T, 2 * W), F32)
    column = ((T, HEAD_DIM), F32)
    smem = pl.BlockSpec(memory_space=pltpu.SMEM)
    vmem = pl.BlockSpec(memory_space=pltpu.VMEM)
    small = pltpu.CompilerParams(vmem_limit_bytes=6 * 2**20)

    held, x, g = pl.pallas_call(
        load_kernel,
        out_shape=tuple(pltpu.VMEM((rows, W), BF16) for rows in (T + PAD, T, T)),
        in_specs=[smem] + [pl.BlockSpec(memory_space=pl.ANY)] * 3,
        out_specs=(vmem,) * 3,
        scratch_shapes=[pltpu.SemaphoreType.DMA((3,))],
        compiler_params=small,
    )(fetch_slot, *(in_hbm(a) for a in (mirror_store, section_input, section_grad)))
    fetched = mirror(held)
    base, away = call(trade_kernel, [tile, tile], place, x, g)
    base_twin = swap(away, "c")

    route = []
    for r in range(16):
        part, group = divmod(r // 2, 4)
        route.append((r, 4 * group + 2 * part + r % 2))
    first = lax.ppermute(keyval_w, TEN, route)
    twin = swap(first, "c")

    (spread,) = call(
        spread_kernel, [((8, 3, T, W), BF16)], place, base, base_twin, fetched, after=(first,)
    )
    own = exchange(spread)
    wq2, wo2 = swap(wq, "c"), swap(wo, "c")
    (picked,) = call(pick_kernel, [((8, T, W), BF16)], place, own, flops=6 * 10**9)
    even = swap(picked, "c")

    dmixed, cols = call(
        dmixed_kernel,
        [((T, 2 * W), BF16), ((2, W, D), BF16)],
        place,
        own,
        anywhere=(wo, wo2),
        scratch=[pltpu.VMEM((T, D), BF16), pltpu.SemaphoreType.DMA((2,))],
        flops=10**9,
    )
    xg, inv, kv, kvb, wkv = call(
        keyval_kernel,
        [((T, D), BF16), ((T, 1), F32), column, ((T, HEAD_DIM), BF16), ((HEAD_DIM, D), BF16)],
        place,
        own,
        even,
        gain,
        anywhere=(first, twin),
        after=(dmixed,),
        flops=10**9,
        scratch=[pltpu.VMEM((T, W), F32), pltpu.SemaphoreType.DMA((2,))],
    )
    q, rows = call(
        queries_kernel,
        [wide, ((2, D, W), BF16)],
        place,
        xg,
        inv,
        anywhere=(wq, wq2),
        scratch=[pltpu.SemaphoreType.DMA((2,))],
        flops=10**9,
    )
    mixed, dq, mine, away = call(
        attend_kernel,
        [((T, 2 * W), BF16), wide, column, ((T, HEAD_DIM), BF16)],
        place,
        kvb,
        swap(kvb, "yl"),
        q,
        dmixed,
    )
    terms, x_late = call(
        terms_kernel,
        [((8, 2, T, W), BF16), tile],
        place,
        own,
        even,
        gain,
        wkv,
        rows,
        cols,
        inv,
        q,
        kv,
        mixed,
        dq,
        mine,
        swap(away, "yl"),
        x,
        flops=10**9,
    )
    evicted = mirror(x_late)
    same, cross = call(finish_kernel, [tile, tile], place, base, base_twin, exchange(terms))
    last = (deliver(same, 0), deliver(cross, 1), evicted)
    return pl.pallas_call(
        store_kernel,
        out_shape=tuple(pltpu.HBM((1, T, W), BF16) for _ in range(3)),
        in_specs=[smem] + [vmem] * 3,
        out_specs=tuple(pl.BlockSpec(memory_space=pl.ANY) for _ in range(3)),
        scratch_shapes=[pltpu.SemaphoreType.DMA((3,))],
        compiler_params=small,
    )(place[0], *(pltpu.with_memory_space_constraint(a, pltpu.VMEM) for a in last))


def solution(mesh):
    fine = Mesh(mesh.devices.reshape(16, 2, 4, 2, 2), SEC + TEN)
    cols = P(SEC, None, TEN)
    return jax.shard_map(
        body,
        mesh=fine,
        in_specs=(
            cols,
            cols,
            P(SEC, None, None, TEN),
            P(SEC),
            P(SEC, None),
            cols,
            P(SEC, TEN, None),
            P(SEC, TEN, None),
        ),
        out_specs=(cols, cols, cols),
        check_vma=False,
    )
```

```python
import jax
import jax.numpy as jnp
from jax import lax
from jax.experimental import pallas as pl
from jax.experimental.pallas import tpu as pltpu
from jax.sharding import Mesh, PartitionSpec as P

HEAD_DIM = 128
EPS = 1e-05
SCALE = HEAD_DIM ** (-0.5)
D = 4096
T = 128
W = 256
N = D // W
PAD = 16

SEC = ("z", "yh")
TEN = ("x", "yl", "c")
F32 = jnp.float32
BF16 = jnp.bfloat16
NT = (((1,), (1,)), ((), ()))
TN = (((0,), (0,)), ((), ()))


def dot(a, b, dims=(((1,), (0,)), ((), ()))):
    return lax.dot_general(a, b, dims, preferred_element_type=F32)


def call(kernel, outs, place, *args, after=(), anywhere=(), scratch=(), flops=0):
    nbytes = sum(a.size * a.dtype.itemsize for a in args)
    n = len(args) + len(anywhere)

    def ordered(core, low, *refs):
        kernel(core, low, *refs[:n], *refs[n + len(after) :])

    return pl.pallas_call(
        ordered,
        out_shape=tuple(pltpu.VMEM(s, d) for s, d in outs),
        in_specs=[pl.BlockSpec(memory_space=pltpu.SMEM)] * 2
        + [pl.BlockSpec(memory_space=pltpu.VMEM)] * len(args)
        + [pl.BlockSpec(memory_space=pl.ANY)] * (len(anywhere) + len(after)),
        out_specs=tuple(pl.BlockSpec(memory_space=pltpu.VMEM) for _ in outs),
        scratch_shapes=list(scratch),
        compiler_params=pltpu.CompilerParams(vmem_limit_bytes=16 * 2**20),
        cost_estimate=pl.CostEstimate(flops=flops, bytes_accessed=nbytes, transcendentals=0),
    )(*place, *(pltpu.with_memory_space_constraint(a, pltpu.VMEM) for a in args), *anywhere, *after)


def in_hbm(a):
    return pltpu.with_memory_space_constraint(a, pltpu.HBM)


def at(index, size=W):
    return pl.ds(pl.multiple_of(index * size, size), size)


def load_kernel(slot, store, x, g, held, x_out, g_out, sems):
    copies = [
        pltpu.make_async_copy(store.at[0, slot[0]], held.at[:T, :], sems.at[0]),
        pltpu.make_async_copy(x.at[0], x_out, sems.at[1]),
        pltpu.make_async_copy(g.at[0], g_out, sems.at[2]),
    ]
    for copy in copies:
        copy.start()
    held[T:, :] = jnp.zeros((PAD, W), BF16)
    for copy in copies:
        copy.wait()


def trade_kernel(core, low, x, g, base, away):
    @pl.when(core[0] == 0)
    def _():
        base[...] = x[...]
        away[...] = g[...]

    @pl.when(core[0] == 1)
    def _():
        base[...] = g[...]
        away[...] = x[...]


def spread_kernel(core, low, base, twin, fetched, x, out, x_out):
    x_out[...] = x[...]
    for j in range(8):
        out[j, core[0]] = base[...]
        out[j, 1 - core[0]] = twin[...]
        out[j, 2] = fetched[:T, :]


def pick_kernel(core, low, own, out):
    out[...] = own[:, 2]


def keyval_kernel(
    core, low, own, even, gain, first, twin, xg, inv_out, kv_out, kvb_out, wkv, squares, sems
):
    half = first.shape[0]
    copies = []
    for i, (ref, side) in enumerate(((first, core[0]), (twin, 1 - core[0]))):
        copies.append(pltpu.make_async_copy(ref, wkv.at[at(side, half), :], sems.at[i]))
        copies[i].start()

    def scaled(left, right):
        total = jnp.zeros((T, W), F32)
        for j in range(8):
            for side, block in enumerate((left(j), right(j))):
                here = slice((2 * j + side) * W, (2 * j + side + 1) * W)
                wide = block.astype(F32)
                total += wide * wide
                xg[:, here] = (wide * gain[:, here]).astype(BF16)
        squares[...] = total

    @pl.when(core[0] == 0)
    def _():
        scaled(lambda j: own[j, 0], lambda j: own[j, 1])

    @pl.when(core[0] == 1)
    def _():
        scaled(lambda j: even[j], lambda j: own[j, 2])

    inv = lax.rsqrt(jnp.sum(squares[...], axis=-1, keepdims=True) * (1.0 / D) + EPS)
    inv_out[...] = inv
    for copy in copies:
        copy.wait()
    kv = dot(xg[...], wkv[...], NT) * inv
    kv_out[...] = kv
    kvb_out[...] = kv.astype(BF16)


def loads(weights, refs, sems):
    copies = [pltpu.make_async_copy(w, refs.at[i], sems.at[i]) for i, w in enumerate(weights)]
    for copy in copies:
        copy.start()
    return copies


def queries_kernel(core, low, xg, inv, wq, wq2, q_out, rows, sems):
    for i, load in enumerate(loads((wq, wq2), rows, sems)):
        load.wait()
        q_out[:, i * W : (i + 1) * W] = dot(xg[...], rows[i]) * inv[...]


def dmixed_kernel(core, low, own, wo, wo2, dmixed, cols, g, sems):
    copies = loads((wo, wo2), cols, sems)

    @pl.when(core[0] == 1)
    def _():
        for r in range(N):
            g[:, r * W : (r + 1) * W] = own[r // 2, r % 2]

    for i, copy in enumerate(copies):
        copy.wait()

        @pl.when(core[0] == 1)
        def _(i=i):
            dmixed[:, i * W : (i + 1) * W] = dot(g[...], cols[i], NT).astype(BF16)


def softmax(qb, k):
    row = lax.broadcasted_iota(jnp.int32, (T, T), 0)
    col = lax.broadcasted_iota(jnp.int32, (T, T), 1)
    s = jnp.where(row >= col, dot(qb, k, NT) * SCALE, F32(-1e30))
    e = jnp.exp(s - jnp.max(s, axis=-1, keepdims=True))
    return e / jnp.sum(e, axis=-1, keepdims=True)


def attend_kernel(core, low, kvb, got, q, dmixed, mixed, dq_out, own_out, away_out):
    keys = low[0] == 0
    k = jnp.where(keys, kvb[...], got[...])
    v = jnp.where(keys, got[...], kvb[...])

    @pl.when(core[0] == 0)
    def _():
        for h in range(4):
            lanes = slice(h * HEAD_DIM, (h + 1) * HEAD_DIM)
            p = softmax(q[:, lanes].astype(BF16), k)
            mixed[:, lanes] = dot(p.astype(BF16), v).astype(BF16)
        away_out[...] = jnp.zeros((T, HEAD_DIM), BF16)

    @pl.when(core[0] == 1)
    def _():
        dk, dv = 0.0, 0.0
        for h in range(4):
            lanes = slice(h * HEAD_DIM, (h + 1) * HEAD_DIM)
            qb, dm = q[:, lanes].astype(BF16), dmixed[:, lanes]
            p = softmax(qb, k)
            dprob = dot(dm, v, NT)
            dscore = (p * (dprob - jnp.sum(p * dprob, axis=-1, keepdims=True))).astype(BF16)
            dq_out[:, lanes] = dot(dscore, k) * SCALE
            dk += dot(dscore, qb, TN)
            dv += dot(p.astype(BF16), dm, TN)
        dk = dk * SCALE
        own_out[...] = jnp.where(keys, dk, dv)
        away_out[...] = jnp.where(keys, dv, dk).astype(BF16)


def products_kernel(core, low, rows, cols, mixed, dq, inv, part):
    @pl.when(core[0] == 0)
    def _():
        for r in range(N):
            here = slice(r * W, (r + 1) * W)
            part[r] = dot(mixed[:, :W], cols[0, :, here]) + dot(mixed[:, W:], cols[1, :, here])

    @pl.when(core[0] == 1)
    def _():
        dqs = (dq[...] * inv[...]).astype(BF16)
        for r in range(N):
            here = slice(r * W, (r + 1) * W)
            part[r] = dot(dqs[:, :W], rows[0, here, :], NT) + dot(dqs[:, W:], rows[1, here, :], NT)


def terms_kernel(core, low, part, own, even, gain, wkv, inv, q, kv, dq, mine, got, out):
    @pl.when(core[0] == 0)
    def _():
        for r in range(N):
            out[r // 2, r % 2] = part[r].astype(BF16)

    @pl.when(core[0] == 1)
    def _():
        r_norm = inv[...]
        dkv = mine[...] + got[...].astype(F32)
        share = jnp.sum(dq[...] * q[...], axis=-1, keepdims=True)
        share += jnp.sum(dkv * kv[...], axis=-1, keepdims=True)
        coef = r_norm * r_norm * share * (1.0 / D)
        dkvs = (dkv * r_norm).astype(BF16)
        for r in range(N):
            here = slice(r * W, (r + 1) * W)
            f = own[r // 2, 2] if r % 2 else even[r // 2]
            term = part[r] + dot(dkvs, wkv[:, here])
            out[r // 2, r % 2] = (term * gain[:, here] - coef * f.astype(F32)).astype(BF16)


def finish_kernel(core, low, base, twin, got, same, cross):
    for start, side, out in ((base, core[0], same), (twin, 1 - core[0], cross)):
        total = start[...].astype(F32)
        for j in range(8):
            total += got[j, side].astype(F32)
        out[...] = total.astype(BF16)


def store_kernel(core, same, cross, evicted, y_out, dx_out, evicted_out, sems):
    last = pltpu.make_async_copy(evicted, evicted_out.at[0], sems.at[2])
    last.start()

    @pl.when(core[0] == 0)
    def _():
        pltpu.make_async_copy(same, y_out.at[0], sems.at[0]).start()
        pltpu.make_async_copy(cross, dx_out.at[0], sems.at[1]).start()

    @pl.when(core[0] == 1)
    def _():
        pltpu.make_async_copy(cross, y_out.at[0], sems.at[0]).start()
        pltpu.make_async_copy(same, dx_out.at[0], sems.at[1]).start()

    pltpu.make_async_copy(same, y_out.at[0], sems.at[0]).wait()
    pltpu.make_async_copy(cross, dx_out.at[0], sems.at[1]).wait()
    last.wait()


def deliver(block, cross):
    route = []
    for i in range(32):
        route.append((2 * i, 2 * ((i + 1) % 32) + cross))
        route.append((2 * i + 1, 2 * ((i - 1) % 32) + 1 - cross))
    return lax.ppermute(block, SEC + ("c",), route)


def mirror(block):
    return lax.ppermute(block, SEC, [(i, 31 - i) for i in range(32)])


def swap(block, axis):
    return lax.ppermute(block, axis, [(0, 1), (1, 0)])


def exchange(parts):
    return lax.all_to_all(parts, ("x", "yl"), 0, 0, tiled=True)


def body(section_input, section_grad, mirror_store, fetch_slot, norm_gain, w_query, w_keyval, w_output):
    gain, wq, wo, keyval_w = norm_gain, w_query[0], w_output[0], w_keyval[0]
    place = [lax.axis_index(a).astype(jnp.int32).reshape(1) for a in ("c", "yl")]
    tile = ((T, W), BF16)
    wide = ((T, 2 * W), F32)
    column = ((T, HEAD_DIM), F32)
    smem = pl.BlockSpec(memory_space=pltpu.SMEM)
    vmem = pl.BlockSpec(memory_space=pltpu.VMEM)
    small = pltpu.CompilerParams(vmem_limit_bytes=6 * 2**20)

    held, x, g = pl.pallas_call(
        load_kernel,
        out_shape=tuple(pltpu.VMEM((rows, W), BF16) for rows in (T + PAD, T, T)),
        in_specs=[smem] + [pl.BlockSpec(memory_space=pl.ANY)] * 3,
        out_specs=(vmem,) * 3,
        scratch_shapes=[pltpu.SemaphoreType.DMA((3,))],
        compiler_params=small,
    )(fetch_slot, *(in_hbm(a) for a in (mirror_store, section_input, section_grad)))
    fetched = mirror(held)
    base, away = call(trade_kernel, [tile, tile], place, x, g)
    base_twin = swap(away, "c")

    route = []
    for r in range(16):
        part, group = divmod(r // 2, 4)
        route.append((r, 4 * group + 2 * part + r % 2))
    first = lax.ppermute(keyval_w, TEN, route)
    twin = swap(first, "c")

    spread, x_late = call(
        spread_kernel,
        [((8, 3, T, W), BF16), tile],
        place,
        base,
        base_twin,
        fetched,
        x,
        after=(first,),
    )
    own = exchange(spread)
    evicted = mirror(x_late)
    wq2, wo2 = swap(wq, "c"), swap(wo, "c")
    (picked,) = call(pick_kernel, [((8, T, W), BF16)], place, own, flops=30 * 10**9, after=(evicted,))
    even = swap(picked, "c")

    dmixed, cols = call(
        dmixed_kernel,
        [((T, 2 * W), BF16), ((2, W, D), BF16)],
        place,
        own,
        anywhere=(wo, wo2),
        scratch=[pltpu.VMEM((T, D), BF16), pltpu.SemaphoreType.DMA((2,))],
        flops=10**9,
    )
    xg, inv, kv, kvb, wkv = call(
        keyval_kernel,
        [((T, D), BF16), ((T, 1), F32), column, ((T, HEAD_DIM), BF16), ((HEAD_DIM, D), BF16)],
        place,
        own,
        even,
        gain,
        anywhere=(first, twin),
        after=(dmixed,),
        flops=10**9,
        scratch=[pltpu.VMEM((T, W), F32), pltpu.SemaphoreType.DMA((2,))],
    )
    q, rows = call(
        queries_kernel,
        [wide, ((2, D, W), BF16)],
        place,
        xg,
        inv,
        anywhere=(wq, wq2),
        scratch=[pltpu.SemaphoreType.DMA((2,))],
        flops=10**9,
    )
    mixed, dq, mine, away = call(
        attend_kernel,
        [((T, 2 * W), BF16), wide, column, ((T, HEAD_DIM), BF16)],
        place,
        kvb,
        swap(kvb, "yl"),
        q,
        dmixed,
    )
    (part,) = call(
        products_kernel, [((N, T, W), F32)], place, rows, cols, mixed, dq, inv, flops=10**9
    )
    (terms,) = call(
        terms_kernel,
        [((8, 2, T, W), BF16)],
        place,
        part,
        own,
        even,
        gain,
        wkv,
        inv,
        q,
        kv,
        dq,
        mine,
        swap(away, "yl"),
    )
    same, cross = call(finish_kernel, [tile, tile], place, base, base_twin, exchange(terms))
    last = (deliver(same, 0), deliver(cross, 1), evicted)
    return pl.pallas_call(
        store_kernel,
        out_shape=tuple(pltpu.HBM((1, T, W), BF16) for _ in range(3)),
        in_specs=[smem] + [vmem] * 3,
        out_specs=tuple(pl.BlockSpec(memory_space=pl.ANY) for _ in range(3)),
        scratch_shapes=[pltpu.SemaphoreType.DMA((3,))],
        compiler_params=small,
    )(place[0], *(pltpu.with_memory_space_constraint(a, pltpu.VMEM) for a in last))


def solution(mesh):
    fine = Mesh(mesh.devices.reshape(16, 2, 4, 2, 2), SEC + TEN)
    cols = P(SEC, None, TEN)
    return jax.shard_map(
        body,
        mesh=fine,
        in_specs=(
            cols,
            cols,
            P(SEC, None, None, TEN),
            P(SEC),
            P(SEC, None),
            cols,
            P(SEC, TEN, None),
            P(SEC, TEN, None),
        ),
        out_specs=(cols, cols, cols),
        check_vma=False,
    )
```

```python
import jax
import jax.numpy as jnp
from jax import lax
from jax.experimental import pallas as pl
from jax.experimental.pallas import tpu as pltpu
from jax.sharding import Mesh, PartitionSpec as P

HEAD_DIM = 128
EPS = 1e-05
SCALE = HEAD_DIM ** (-0.5)
D = 4096
T = 128
W = 256
N = D // W
PAD = 16

SEC = ("z", "yh")
TEN = ("x", "yl", "c")
F32 = jnp.float32
BF16 = jnp.bfloat16
NT = (((1,), (1,)), ((), ()))
TN = (((0,), (0,)), ((), ()))


def dot(a, b, dims=(((1,), (0,)), ((), ()))):
    return lax.dot_general(a, b, dims, preferred_element_type=F32)


def call(kernel, outs, place, *args, after=(), anywhere=(), scratch=(), flops=0):
    nbytes = sum(a.size * a.dtype.itemsize for a in args)
    n = len(args) + len(anywhere)

    def ordered(core, low, *refs):
        kernel(core, low, *refs[:n], *refs[n + len(after) :])

    return pl.pallas_call(
        ordered,
        out_shape=tuple(pltpu.VMEM(s, d) for s, d in outs),
        in_specs=[pl.BlockSpec(memory_space=pltpu.SMEM)] * 2
        + [pl.BlockSpec(memory_space=pltpu.VMEM)] * len(args)
        + [pl.BlockSpec(memory_space=pl.ANY)] * (len(anywhere) + len(after)),
        out_specs=tuple(pl.BlockSpec(memory_space=pltpu.VMEM) for _ in outs),
        scratch_shapes=list(scratch),
        compiler_params=pltpu.CompilerParams(vmem_limit_bytes=16 * 2**20),
        cost_estimate=pl.CostEstimate(flops=flops, bytes_accessed=nbytes, transcendentals=0),
    )(*place, *(pltpu.with_memory_space_constraint(a, pltpu.VMEM) for a in args), *anywhere, *after)


def in_hbm(a):
    return pltpu.with_memory_space_constraint(a, pltpu.HBM)


def at(index, size=W):
    return pl.ds(pl.multiple_of(index * size, size), size)


def load_kernel(slot, store, x, g, held, x_out, g_out, sems):
    copies = [
        pltpu.make_async_copy(store.at[0, slot[0]], held.at[:T, :], sems.at[0]),
        pltpu.make_async_copy(x.at[0], x_out, sems.at[1]),
        pltpu.make_async_copy(g.at[0], g_out, sems.at[2]),
    ]
    for copy in copies:
        copy.start()
    held[T:, :] = jnp.zeros((PAD, W), BF16)
    for copy in copies:
        copy.wait()


def trade_kernel(core, low, x, g, base, away):
    @pl.when(core[0] == 0)
    def _():
        base[...] = x[...]
        away[...] = g[...]

    @pl.when(core[0] == 1)
    def _():
        base[...] = g[...]
        away[...] = x[...]


def spread_kernel(core, low, base, twin, fetched, x, out, x_out):
    x_out[...] = x[...]
    for j in range(8):
        out[j, core[0]] = base[...]
        out[j, 1 - core[0]] = twin[...]
        out[j, 2] = fetched[:T, :]


def pick_kernel(core, low, own, out):
    out[...] = own[:, 2]


def keyval_kernel(
    core, low, own, even, gain, first, twin, xg, inv_out, kv_out, kvb_out, wkv, squares, sems
):
    half = first.shape[0]
    copies = []
    for i, (ref, side) in enumerate(((first, core[0]), (twin, 1 - core[0]))):
        copies.append(pltpu.make_async_copy(ref, wkv.at[at(side, half), :], sems.at[i]))
        copies[i].start()

    def scaled(left, right):
        total = jnp.zeros((T, W), F32)
        for j in range(8):
            for side, block in enumerate((left(j), right(j))):
                here = slice((2 * j + side) * W, (2 * j + side + 1) * W)
                wide = block.astype(F32)
                total += wide * wide
                xg[:, here] = (wide * gain[:, here]).astype(BF16)
        squares[...] = total

    @pl.when(core[0] == 0)
    def _():
        scaled(lambda j: own[j, 0], lambda j: own[j, 1])

    @pl.when(core[0] == 1)
    def _():
        scaled(lambda j: even[j], lambda j: own[j, 2])

    inv = lax.rsqrt(jnp.sum(squares[...], axis=-1, keepdims=True) * (1.0 / D) + EPS)
    inv_out[...] = inv
    for copy in copies:
        copy.wait()
    kv = dot(xg[...], wkv[...], NT) * inv
    kv_out[...] = kv
    kvb_out[...] = kv.astype(BF16)


def loads(weights, refs, sems):
    copies = [pltpu.make_async_copy(w, refs.at[i], sems.at[i]) for i, w in enumerate(weights)]
    for copy in copies:
        copy.start()
    return copies


def queries_kernel(core, low, xg, inv, wq, wq2, q_out, rows, sems):
    for i, load in enumerate(loads((wq, wq2), rows, sems)):
        load.wait()
        q_out[:, i * W : (i + 1) * W] = dot(xg[...], rows[i]) * inv[...]


def dmixed_kernel(core, low, own, wo, wo2, dmixed, cols, g, sems):
    copies = loads((wo, wo2), cols, sems)

    @pl.when(core[0] == 1)
    def _():
        for r in range(N):
            g[:, r * W : (r + 1) * W] = own[r // 2, r % 2]

    for i, copy in enumerate(copies):
        copy.wait()

        @pl.when(core[0] == 1)
        def _(i=i):
            dmixed[:, i * W : (i + 1) * W] = dot(g[...], cols[i], NT).astype(BF16)


def stacked(x):
    return jnp.concatenate([x[:, h * HEAD_DIM : (h + 1) * HEAD_DIM] for h in range(4)], axis=0)


def softmax(qb, k):
    row = lax.broadcasted_iota(jnp.int32, (4, T, T), 1).reshape(4 * T, T)
    col = lax.broadcasted_iota(jnp.int32, (4 * T, T), 1)
    s = jnp.where(row >= col, dot(qb, k, NT) * SCALE, F32(-1e30))
    e = jnp.exp(s - jnp.max(s, axis=-1, keepdims=True))
    return e / jnp.sum(e, axis=-1, keepdims=True)


def attend_kernel(core, low, kvb, got, q, dmixed, mixed, dq_out, own_out, away_out):
    keys = low[0] == 0
    k = jnp.where(keys, kvb[...], got[...])
    v = jnp.where(keys, got[...], kvb[...])
    qb = stacked(q[...]).astype(BF16)
    p = softmax(qb, k)
    pb = p.astype(BF16)

    @pl.when(core[0] == 0)
    def _():
        out = dot(pb, v).astype(BF16)
        for h in range(4):
            mixed[:, h * HEAD_DIM : (h + 1) * HEAD_DIM] = out[h * T : (h + 1) * T, :]
        away_out[...] = jnp.zeros((T, HEAD_DIM), BF16)

    @pl.when(core[0] == 1)
    def _():
        dm = stacked(dmixed[...])
        dprob = dot(dm, v, NT)
        dscore = (p * (dprob - jnp.sum(p * dprob, axis=-1, keepdims=True))).astype(BF16)
        out = dot(dscore, k) * SCALE
        for h in range(4):
            dq_out[:, h * HEAD_DIM : (h + 1) * HEAD_DIM] = out[h * T : (h + 1) * T, :]
        dk = dot(dscore, qb, TN) * SCALE
        dv = dot(pb, dm, TN)
        own_out[...] = jnp.where(keys, dk, dv)
        away_out[...] = jnp.where(keys, dv, dk).astype(BF16)


def products_kernel(core, low, rows, cols, mixed, dq, inv, part):
    @pl.when(core[0] == 0)
    def _():
        for r in range(N):
            here = slice(r * W, (r + 1) * W)
            part[r] = dot(mixed[:, :W], cols[0, :, here]) + dot(mixed[:, W:], cols[1, :, here])

    @pl.when(core[0] == 1)
    def _():
        dqs = (dq[...] * inv[...]).astype(BF16)
        for r in range(N):
            here = slice(r * W, (r + 1) * W)
            part[r] = dot(dqs[:, :W], rows[0, here, :], NT) + dot(dqs[:, W:], rows[1, here, :], NT)


def terms_kernel(core, low, part, own, even, gain, wkv, inv, q, kv, dq, mine, got, out):
    @pl.when(core[0] == 0)
    def _():
        for r in range(N):
            out[r // 2, r % 2] = part[r].astype(BF16)

    @pl.when(core[0] == 1)
    def _():
        r_norm = inv[...]
        dkv = mine[...] + got[...].astype(F32)
        share = jnp.sum(dq[...] * q[...], axis=-1, keepdims=True)
        share += jnp.sum(dkv * kv[...], axis=-1, keepdims=True)
        coef = r_norm * r_norm * share * (1.0 / D)
        dkvs = (dkv * r_norm).astype(BF16)
        for r in range(N):
            here = slice(r * W, (r + 1) * W)
            f = own[r // 2, 2] if r % 2 else even[r // 2]
            term = part[r] + dot(dkvs, wkv[:, here])
            out[r // 2, r % 2] = (term * gain[:, here] - coef * f.astype(F32)).astype(BF16)


def finish_kernel(core, low, base, twin, got, same, cross):
    for start, side, out in ((base, core[0], same), (twin, 1 - core[0], cross)):
        total = start[...].astype(F32)
        for j in range(8):
            total += got[j, side].astype(F32)
        out[...] = total.astype(BF16)


def store_kernel(core, same, cross, evicted, y_out, dx_out, evicted_out, sems):
    last = pltpu.make_async_copy(evicted, evicted_out.at[0], sems.at[2])
    last.start()

    @pl.when(core[0] == 0)
    def _():
        pltpu.make_async_copy(same, y_out.at[0], sems.at[0]).start()
        pltpu.make_async_copy(cross, dx_out.at[0], sems.at[1]).start()

    @pl.when(core[0] == 1)
    def _():
        pltpu.make_async_copy(cross, y_out.at[0], sems.at[0]).start()
        pltpu.make_async_copy(same, dx_out.at[0], sems.at[1]).start()

    pltpu.make_async_copy(same, y_out.at[0], sems.at[0]).wait()
    pltpu.make_async_copy(cross, dx_out.at[0], sems.at[1]).wait()
    last.wait()


def deliver(block, cross):
    route = []
    for i in range(32):
        route.append((2 * i, 2 * ((i + 1) % 32) + cross))
        route.append((2 * i + 1, 2 * ((i - 1) % 32) + 1 - cross))
    return lax.ppermute(block, SEC + ("c",), route)


def mirror(block):
    return lax.ppermute(block, SEC, [(i, 31 - i) for i in range(32)])


def swap(block, axis):
    return lax.ppermute(block, axis, [(0, 1), (1, 0)])


def exchange(parts):
    return lax.all_to_all(parts, ("x", "yl"), 0, 0, tiled=True)


def body(section_input, section_grad, mirror_store, fetch_slot, norm_gain, w_query, w_keyval, w_output):
    gain, wq, wo, keyval_w = norm_gain, w_query[0], w_output[0], w_keyval[0]
    place = [lax.axis_index(a).astype(jnp.int32).reshape(1) for a in ("c", "yl")]
    tile = ((T, W), BF16)
    wide = ((T, 2 * W), F32)
    column = ((T, HEAD_DIM), F32)
    smem = pl.BlockSpec(memory_space=pltpu.SMEM)
    vmem = pl.BlockSpec(memory_space=pltpu.VMEM)
    small = pltpu.CompilerParams(vmem_limit_bytes=6 * 2**20)

    held, x, g = pl.pallas_call(
        load_kernel,
        out_shape=tuple(pltpu.VMEM((rows, W), BF16) for rows in (T + PAD, T, T)),
        in_specs=[smem] + [pl.BlockSpec(memory_space=pl.ANY)] * 3,
        out_specs=(vmem,) * 3,
        scratch_shapes=[pltpu.SemaphoreType.DMA((3,))],
        compiler_params=small,
    )(fetch_slot, *(in_hbm(a) for a in (mirror_store, section_input, section_grad)))
    fetched = mirror(held)
    base, away = call(trade_kernel, [tile, tile], place, x, g)
    base_twin = swap(away, "c")

    route = []
    for r in range(16):
        part, group = divmod(r // 2, 4)
        route.append((r, 4 * group + 2 * part + r % 2))
    first = lax.ppermute(keyval_w, TEN, route)
    twin = swap(first, "c")

    spread, x_late = call(
        spread_kernel,
        [((8, 3, T, W), BF16), tile],
        place,
        base,
        base_twin,
        fetched,
        x,
        after=(first,),
    )
    own = exchange(spread)
    evicted = mirror(x_late)
    wq2, wo2 = swap(wq, "c"), swap(wo, "c")
    (picked,) = call(pick_kernel, [((8, T, W), BF16)], place, own, flops=30 * 10**9, after=(evicted,))
    even = swap(picked, "c")

    dmixed, cols = call(
        dmixed_kernel,
        [((T, 2 * W), BF16), ((2, W, D), BF16)],
        place,
        own,
        anywhere=(wo, wo2),
        scratch=[pltpu.VMEM((T, D), BF16), pltpu.SemaphoreType.DMA((2,))],
        flops=10**9,
    )
    xg, inv, kv, kvb, wkv = call(
        keyval_kernel,
        [((T, D), BF16), ((T, 1), F32), column, ((T, HEAD_DIM), BF16), ((HEAD_DIM, D), BF16)],
        place,
        own,
        even,
        gain,
        anywhere=(first, twin),
        after=(dmixed,),
        flops=10**9,
        scratch=[pltpu.VMEM((T, W), F32), pltpu.SemaphoreType.DMA((2,))],
    )
    q, rows = call(
        queries_kernel,
        [wide, ((2, D, W), BF16)],
        place,
        xg,
        inv,
        anywhere=(wq, wq2),
        scratch=[pltpu.SemaphoreType.DMA((2,))],
        flops=10**9,
    )
    mixed, dq, mine, away = call(
        attend_kernel,
        [((T, 2 * W), BF16), wide, column, ((T, HEAD_DIM), BF16)],
        place,
        kvb,
        swap(kvb, "yl"),
        q,
        dmixed,
    )
    (part,) = call(
        products_kernel, [((N, T, W), F32)], place, rows, cols, mixed, dq, inv, flops=10**9
    )
    (terms,) = call(
        terms_kernel,
        [((8, 2, T, W), BF16)],
        place,
        part,
        own,
        even,
        gain,
        wkv,
        inv,
        q,
        kv,
        dq,
        mine,
        swap(away, "yl"),
    )
    same, cross = call(finish_kernel, [tile, tile], place, base, base_twin, exchange(terms))
    last = (deliver(same, 0), deliver(cross, 1), evicted)
    return pl.pallas_call(
        store_kernel,
        out_shape=tuple(pltpu.HBM((1, T, W), BF16) for _ in range(3)),
        in_specs=[smem] + [vmem] * 3,
        out_specs=tuple(pl.BlockSpec(memory_space=pl.ANY) for _ in range(3)),
        scratch_shapes=[pltpu.SemaphoreType.DMA((3,))],
        compiler_params=small,
    )(place[0], *(pltpu.with_memory_space_constraint(a, pltpu.VMEM) for a in last))


def solution(mesh):
    fine = Mesh(mesh.devices.reshape(16, 2, 4, 2, 2), SEC + TEN)
    cols = P(SEC, None, TEN)
    return jax.shard_map(
        body,
        mesh=fine,
        in_specs=(
            cols,
            cols,
            P(SEC, None, None, TEN),
            P(SEC),
            P(SEC, None),
            cols,
            P(SEC, TEN, None),
            P(SEC, TEN, None),
        ),
        out_specs=(cols, cols, cols),
        check_vma=False,
    )
```

```python
import jax
import jax.numpy as jnp
from jax import lax
from jax.experimental import pallas as pl
from jax.experimental.pallas import tpu as pltpu
from jax.sharding import Mesh, PartitionSpec as P

HEAD_DIM = 128
EPS = 1e-05
SCALE = HEAD_DIM ** (-0.5)
D = 4096
T = 128
W = 256
N = D // W
PAD = 16

SEC = ("z", "yh")
TEN = ("x", "yl", "c")
F32 = jnp.float32
BF16 = jnp.bfloat16
NT = (((1,), (1,)), ((), ()))
TN = (((0,), (0,)), ((), ()))


def dot(a, b, dims=(((1,), (0,)), ((), ()))):
    return lax.dot_general(a, b, dims, preferred_element_type=F32)


def call(kernel, outs, place, *args, after=(), anywhere=(), scratch=(), flops=0):
    nbytes = sum(a.size * a.dtype.itemsize for a in args)
    n = len(args) + len(anywhere)

    def ordered(core, low, *refs):
        kernel(core, low, *refs[:n], *refs[n + len(after) :])

    return pl.pallas_call(
        ordered,
        out_shape=tuple(pltpu.VMEM(s, d) for s, d in outs),
        in_specs=[pl.BlockSpec(memory_space=pltpu.SMEM)] * 2
        + [pl.BlockSpec(memory_space=pltpu.VMEM)] * len(args)
        + [pl.BlockSpec(memory_space=pl.ANY)] * (len(anywhere) + len(after)),
        out_specs=tuple(pl.BlockSpec(memory_space=pltpu.VMEM) for _ in outs),
        scratch_shapes=list(scratch),
        compiler_params=pltpu.CompilerParams(vmem_limit_bytes=16 * 2**20),
        cost_estimate=pl.CostEstimate(flops=flops, bytes_accessed=nbytes, transcendentals=0),
    )(*place, *(pltpu.with_memory_space_constraint(a, pltpu.VMEM) for a in args), *anywhere, *after)


def in_hbm(a):
    return pltpu.with_memory_space_constraint(a, pltpu.HBM)


def at(index, size=W):
    return pl.ds(pl.multiple_of(index * size, size), size)


def load_kernel(x, g, x_out, g_out, sems):
    copies = [
        pltpu.make_async_copy(x.at[0], x_out, sems.at[0]),
        pltpu.make_async_copy(g.at[0], g_out, sems.at[1]),
    ]
    for copy in copies:
        copy.start()
    for copy in copies:
        copy.wait()


def trade_kernel(core, low, x, g, base, away):
    @pl.when(core[0] == 0)
    def _():
        base[...] = x[...]
        away[...] = g[...]

    @pl.when(core[0] == 1)
    def _():
        base[...] = g[...]
        away[...] = x[...]


def spread_kernel(core, base, twin, fetched, x, _, out, x_out, sem):
    copies = []
    for j in range(8):
        for i, ref in ((core[0], base), (1 - core[0], twin), (2, fetched.at[:T, :])):
            copies.append(pltpu.make_async_copy(ref, out.at[j, i], sem.at[len(copies)]))
            copies[-1].start()
    x_out[...] = x[...]
    for copy in copies:
        copy.wait()


def pick_kernel(core, low, own, out):
    out[...] = own[:, 2]


def keyval_kernel(
    core, low, own, even, gain, first, twin, xg, inv_out, kv_out, kvb_out, wkv, squares, sems
):
    half = first.shape[0]
    copies = []
    for i, (ref, side) in enumerate(((first, core[0]), (twin, 1 - core[0]))):
        copies.append(pltpu.make_async_copy(ref, wkv.at[at(side, half), :], sems.at[i]))
        copies[i].start()

    def scaled(left, right):
        total = jnp.zeros((T, W), F32)
        for j in range(8):
            for side, block in enumerate((left(j), right(j))):
                here = slice((2 * j + side) * W, (2 * j + side + 1) * W)
                wide = block.astype(F32)
                total += wide * wide
                xg[:, here] = (wide * gain[:, here]).astype(BF16)
        squares[...] = total

    @pl.when(core[0] == 0)
    def _():
        scaled(lambda j: own[j, 0], lambda j: own[j, 1])

    @pl.when(core[0] == 1)
    def _():
        scaled(lambda j: even[j], lambda j: own[j, 2])

    inv = lax.rsqrt(jnp.sum(squares[...], axis=-1, keepdims=True) * (1.0 / D) + EPS)
    inv_out[...] = inv
    for copy in copies:
        copy.wait()
    kv = dot(xg[...], wkv[...], NT) * inv
    kv_out[...] = kv
    kvb_out[...] = kv.astype(BF16)


def loads(weights, refs, sems):
    copies = [pltpu.make_async_copy(w, refs.at[i], sems.at[i]) for i, w in enumerate(weights)]
    for copy in copies:
        copy.start()
    return copies


def queries_kernel(core, low, xg, inv, wq, wq2, q_out, rows, sems):
    for i, load in enumerate(loads((wq, wq2), rows, sems)):
        load.wait()
        q_out[:, i * W : (i + 1) * W] = dot(xg[...], rows[i]) * inv[...]


def dmixed_kernel(core, low, own, wo, wo2, dmixed, cols, g, sems):
    copies = loads((wo, wo2), cols, sems)

    @pl.when(core[0] == 1)
    def _():
        for r in range(N):
            g[:, r * W : (r + 1) * W] = own[r // 2, r % 2]

    for i, copy in enumerate(copies):
        copy.wait()

        @pl.when(core[0] == 1)
        def _(i=i):
            dmixed[:, i * W : (i + 1) * W] = dot(g[...], cols[i], NT).astype(BF16)


def stacked(x):
    return jnp.concatenate([x[:, h * HEAD_DIM : (h + 1) * HEAD_DIM] for h in range(4)], axis=0)


def softmax(qb, k):
    row = lax.broadcasted_iota(jnp.int32, (4, T, T), 1).reshape(4 * T, T)
    col = lax.broadcasted_iota(jnp.int32, (4 * T, T), 1)
    s = jnp.where(row >= col, dot(qb, k, NT) * SCALE, F32(-1e30))
    e = jnp.exp(s - jnp.max(s, axis=-1, keepdims=True))
    return e / jnp.sum(e, axis=-1, keepdims=True)


def attend_kernel(core, low, kvb, got, q, dmixed, mixed, dq_out, own_out, away_out):
    keys = low[0] == 0
    k = jnp.where(keys, kvb[...], got[...])
    v = jnp.where(keys, got[...], kvb[...])
    qb = stacked(q[...]).astype(BF16)
    p = softmax(qb, k)
    pb = p.astype(BF16)

    @pl.when(core[0] == 0)
    def _():
        out = dot(pb, v).astype(BF16)
        for h in range(4):
            mixed[:, h * HEAD_DIM : (h + 1) * HEAD_DIM] = out[h * T : (h + 1) * T, :]
        away_out[...] = jnp.zeros((T, HEAD_DIM), BF16)

    @pl.when(core[0] == 1)
    def _():
        dm = stacked(dmixed[...])
        dprob = dot(dm, v, NT)
        dscore = (p * (dprob - jnp.sum(p * dprob, axis=-1, keepdims=True))).astype(BF16)
        out = dot(dscore, k) * SCALE
        for h in range(4):
            dq_out[:, h * HEAD_DIM : (h + 1) * HEAD_DIM] = out[h * T : (h + 1) * T, :]
        dk = dot(dscore, qb, TN) * SCALE
        dv = dot(pb, dm, TN)
        own_out[...] = jnp.where(keys, dk, dv)
        away_out[...] = jnp.where(keys, dv, dk).astype(BF16)


def products_kernel(core, low, rows, cols, mixed, dq, inv, part):
    @pl.when(core[0] == 0)
    def _():
        for r in range(N):
            here = slice(r * W, (r + 1) * W)
            part[r] = dot(mixed[:, :W], cols[0, :, here]) + dot(mixed[:, W:], cols[1, :, here])

    @pl.when(core[0] == 1)
    def _():
        dqs = (dq[...] * inv[...]).astype(BF16)
        for r in range(N):
            here = slice(r * W, (r + 1) * W)
            part[r] = dot(dqs[:, :W], rows[0, here, :], NT) + dot(dqs[:, W:], rows[1, here, :], NT)


def terms_kernel(core, low, part, own, even, gain, wkv, inv, q, kv, dq, mine, got, out):
    @pl.when(core[0] == 0)
    def _():
        for r in range(N):
            out[r // 2, r % 2] = part[r].astype(BF16)

    @pl.when(core[0] == 1)
    def _():
        r_norm = inv[...]
        dkv = mine[...] + got[...].astype(F32)
        share = jnp.sum(dq[...] * q[...], axis=-1, keepdims=True)
        share += jnp.sum(dkv * kv[...], axis=-1, keepdims=True)
        coef = r_norm * r_norm * share * (1.0 / D)
        dkvs = (dkv * r_norm).astype(BF16)
        for r in range(N):
            here = slice(r * W, (r + 1) * W)
            f = own[r // 2, 2] if r % 2 else even[r // 2]
            term = part[r] + dot(dkvs, wkv[:, here])
            out[r // 2, r % 2] = (term * gain[:, here] - coef * f.astype(F32)).astype(BF16)


def finish_kernel(core, low, base, twin, got, same, cross):
    for start, side, out in ((base, core[0], same), (twin, 1 - core[0], cross)):
        total = start[...].astype(F32)
        for j in range(8):
            total += got[j, side].astype(F32)
        out[...] = total.astype(BF16)


def store_kernel(core, same, cross, evicted, y_out, dx_out, evicted_out, sems):
    last = pltpu.make_async_copy(evicted, evicted_out.at[0], sems.at[2])
    last.start()

    @pl.when(core[0] == 0)
    def _():
        pltpu.make_async_copy(same, y_out.at[0], sems.at[0]).start()
        pltpu.make_async_copy(cross, dx_out.at[0], sems.at[1]).start()

    @pl.when(core[0] == 1)
    def _():
        pltpu.make_async_copy(cross, y_out.at[0], sems.at[0]).start()
        pltpu.make_async_copy(same, dx_out.at[0], sems.at[1]).start()

    pltpu.make_async_copy(same, y_out.at[0], sems.at[0]).wait()
    pltpu.make_async_copy(cross, dx_out.at[0], sems.at[1]).wait()
    last.wait()


def deliver(block, cross):
    route = []
    for i in range(32):
        route.append((2 * i, 2 * ((i + 1) % 32) + cross))
        route.append((2 * i + 1, 2 * ((i - 1) % 32) + 1 - cross))
    return lax.ppermute(block, SEC + ("c",), route)


def mirror(block):
    return lax.ppermute(block, SEC, [(i, 31 - i) for i in range(32)])


def swap(block, axis):
    return lax.ppermute(block, axis, [(0, 1), (1, 0)])


def exchange(parts):
    return lax.all_to_all(parts, ("x", "yl"), 0, 0, tiled=True)


def body(section_input, section_grad, mirror_store, fetch_slot, norm_gain, w_query, w_keyval, w_output):
    gain, wq, wo, keyval_w = norm_gain, w_query[0], w_output[0], w_keyval[0]
    place = [lax.axis_index(a).astype(jnp.int32).reshape(1) for a in ("c", "yl")]
    tile = ((T, W), BF16)
    wide = ((T, 2 * W), F32)
    column = ((T, HEAD_DIM), F32)
    smem = pl.BlockSpec(memory_space=pltpu.SMEM)
    vmem = pl.BlockSpec(memory_space=pltpu.VMEM)
    small = pltpu.CompilerParams(vmem_limit_bytes=6 * 2**20)

    held = lax.dynamic_index_in_dim(mirror_store[0], fetch_slot[0], 0, keepdims=False)
    held = jnp.pad(held, ((0, PAD), (0, 0)))
    x, g = pl.pallas_call(
        load_kernel,
        out_shape=tuple(pltpu.VMEM((T, W), BF16) for _ in range(2)),
        in_specs=[pl.BlockSpec(memory_space=pl.ANY)] * 2,
        out_specs=(vmem,) * 2,
        scratch_shapes=[pltpu.SemaphoreType.DMA((2,))],
        compiler_params=small,
    )(*(in_hbm(a) for a in (section_input, section_grad)))
    fetched = mirror(held)
    base, away = call(trade_kernel, [tile, tile], place, x, g)
    base_twin = swap(away, "c")

    route = []
    for r in range(16):
        part, group = divmod(r // 2, 4)
        route.append((r, 4 * group + 2 * part + r % 2))
    first = lax.ppermute(keyval_w, TEN, route)
    twin = swap(first, "c")

    parts = [pltpu.with_memory_space_constraint(a, pltpu.VMEM) for a in (base, base_twin, fetched, x)]
    spread, x_late = pl.pallas_call(
        spread_kernel,
        out_shape=(pltpu.HBM((8, 3, T, W), BF16), pltpu.VMEM((T, W), BF16)),
        in_specs=[smem] + [vmem] * 4 + [pl.BlockSpec(memory_space=pl.ANY)],
        out_specs=(pl.BlockSpec(memory_space=pl.ANY), vmem),
        scratch_shapes=[pltpu.SemaphoreType.DMA((24,))],
        compiler_params=small,
    )(place[0], *parts, first)
    own = exchange(spread)
    evicted = mirror(x_late)
    wq2, wo2 = swap(wq, "c"), swap(wo, "c")
    (picked,) = call(pick_kernel, [((8, T, W), BF16)], place, own, flops=30 * 10**9, after=(evicted,))
    even = swap(picked, "c")

    dmixed, cols = call(
        dmixed_kernel,
        [((T, 2 * W), BF16), ((2, W, D), BF16)],
        place,
        own,
        anywhere=(wo, wo2),
        scratch=[pltpu.VMEM((T, D), BF16), pltpu.SemaphoreType.DMA((2,))],
        flops=10**9,
    )
    xg, inv, kv, kvb, wkv = call(
        keyval_kernel,
        [((T, D), BF16), ((T, 1), F32), column, ((T, HEAD_DIM), BF16), ((HEAD_DIM, D), BF16)],
        place,
        own,
        even,
        gain,
        anywhere=(first, twin),
        after=(dmixed,),
        flops=10**9,
        scratch=[pltpu.VMEM((T, W), F32), pltpu.SemaphoreType.DMA((2,))],
    )
    q, rows = call(
        queries_kernel,
        [wide, ((2, D, W), BF16)],
        place,
        xg,
        inv,
        anywhere=(wq, wq2),
        scratch=[pltpu.SemaphoreType.DMA((2,))],
        flops=10**9,
    )
    mixed, dq, mine, away = call(
        attend_kernel,
        [((T, 2 * W), BF16), wide, column, ((T, HEAD_DIM), BF16)],
        place,
        kvb,
        swap(kvb, "yl"),
        q,
        dmixed,
    )
    (part,) = call(
        products_kernel, [((N, T, W), F32)], place, rows, cols, mixed, dq, inv, flops=10**9
    )
    (terms,) = call(
        terms_kernel,
        [((8, 2, T, W), BF16)],
        place,
        part,
        own,
        even,
        gain,
        wkv,
        inv,
        q,
        kv,
        dq,
        mine,
        swap(away, "yl"),
    )
    same, cross = call(finish_kernel, [tile, tile], place, base, base_twin, exchange(terms))
    last = (deliver(same, 0), deliver(cross, 1), evicted)
    return pl.pallas_call(
        store_kernel,
        out_shape=tuple(pltpu.HBM((1, T, W), BF16) for _ in range(3)),
        in_specs=[smem] + [vmem] * 3,
        out_specs=tuple(pl.BlockSpec(memory_space=pl.ANY) for _ in range(3)),
        scratch_shapes=[pltpu.SemaphoreType.DMA((3,))],
        compiler_params=small,
    )(place[0], *(pltpu.with_memory_space_constraint(a, pltpu.VMEM) for a in last))


def solution(mesh):
    fine = Mesh(mesh.devices.reshape(16, 2, 4, 2, 2), SEC + TEN)
    cols = P(SEC, None, TEN)
    return jax.shard_map(
        body,
        mesh=fine,
        in_specs=(
            cols,
            cols,
            P(SEC, None, None, TEN),
            P(SEC),
            P(SEC, None),
            cols,
            P(SEC, TEN, None),
            P(SEC, TEN, None),
        ),
        out_specs=(cols, cols, cols),
        check_vma=False,
    )
```
